32 devices in a mesh: dp: 8 (over z, y), tensor: 4 (over x, core).
Axes of the slice: x: 2, y: 2, z: 4, core: 2. Of those that a mesh axis runs over, the one named last changes fastest.
Arguments:
- inputs: bfloat16 [4096, 1024], P(('dp', 'tensor')), may hold values from -6 to 6
- cotangent: bfloat16 [4096, 1024], P(('dp', 'tensor')), may hold values from -6 to 6
- mix_gain: bfloat16 [1024], P('dp'), may hold values from 0.25 to 1.75
- query_weight: bfloat16 [1024, 512], P('dp', 'tensor'), may hold values from -0.1875 to 0.1875
- key_weight: bfloat16 [1024, 128], P('dp'), may hold values from -0.1875 to 0.1875
- value_weight: bfloat16 [1024, 128], P('dp'), may hold values from -0.1875 to 0.1875
- attention_out: bfloat16 [1024, 512], P('dp', 'tensor'), may hold values from -3 to 3
- mamba_gate: bfloat16 [1024, 1536], P('dp', 'tensor'), may hold values from -0.1875 to 0.1875
- mamba_input: bfloat16 [1024, 1536], P('dp', 'tensor'), may hold values from -0.1875 to 0.1875
- state_weight: bfloat16 [1024, 256], P('dp'), may hold values from -0.1875 to 0.1875
- step_weight: bfloat16 [1024, 24], P('dp', 'tensor'), may hold values from -0.1875 to 0.1875
- mamba_out: bfloat16 [1024, 1536], P('dp', 'tensor'), may hold values from -0.3125 to 0.3125
- kernel_weight: float32 [4, 1792], replicated, may hold values from -3 to 3
- kernel_bias: float32 [1792], replicated, may hold values from -3 to 3
- decay_log: float32 [24], replicated, may hold values from 0 to 2.77
- step_bias: float32 [24], replicated, may hold values from -4.5 to -2
- skip_weight: float32 [24], replicated, may hold values from 0.5 to 2
- mlp_gain: bfloat16 [1024], P('dp'), may hold values from 0.25 to 1.75
- gate_weight: bfloat16 [1024, 2048], P('dp', 'tensor'), may hold values from -0.1875 to 0.1875
- up_weight: bfloat16 [1024, 2048], P('dp', 'tensor'), may hold values from -0.1875 to 0.1875
- down_weight: bfloat16 [1024, 2048], P('dp', 'tensor'), may hold values from -0.1875 to 0.1875
Outputs:
- output: bfloat16 [4096, 1024], P(('dp', 'tensor'))
- grad_inputs: bfloat16 [4096, 1024], P(('dp', 'tensor'))
- grad_mix_gain: float32 [1024], P(('dp', 'tensor'))
- grad_query_weight: float32 [1024, 512], P('dp', 'tensor')
- grad_key_weight: float32 [1024, 128], P(('dp', 'tensor'))
- grad_value_weight: float32 [1024, 128], P(('dp', 'tensor'))
- grad_attention_out: float32 [1024, 512], P('dp', 'tensor')
- grad_mamba_gate: float32 [1024, 1536], P('dp', 'tensor')
- grad_mamba_input: float32 [1024, 1536], P('dp', 'tensor')
- grad_state_weight: float32 [1024, 256], P(('dp', 'tensor'))
- grad_step_weight: float32 [1024, 24], P('dp', 'tensor')
- grad_mamba_out: float32 [1024, 1536], P('dp', 'tensor')
- grad_kernel_weight: float32 [4, 1792], replicated
- grad_kernel_bias: float32 [1792], replicated
- grad_decay_log: float32 [24], replicated
- grad_step_bias: float32 [24], replicated
- grad_skip_weight: float32 [24], replicated
- grad_mlp_gain: float32 [1024], P(('dp', 'tensor'))
- grad_gate_weight: float32 [1024, 2048], P('dp', 'tensor')
- grad_up_weight: float32 [1024, 2048], P('dp', 'tensor')
- grad_down_weight: float32 [1024, 2048], P('dp', 'tensor')
The draws below stay inside these ranges and needn't reach their ends.
All inputs are finite; a program needn't handle non-finite values.
Results may differ from the reference program's by a relative error of at most 0.02.
Values may be sent and summed in bfloat16 or wider, within the bound.
A program may use at most 128 MiB of HBM per device.

```python
import math
import jax
import jax.numpy as jnp
from jax import lax

D = 1024
HEADS = 8
KV_HEADS = 2
HEAD_DIM = 64
SSM_HEADS = 24
SSM_HEAD_DIM = 64
STATE = 128
FF = 2048
KCONV = 4
SCAN_BLOCK = 128
LEN = 512
TOKENS = 4096
N_TENSOR = 4


def strengthened(values, rng, source, target, blocks, factor):
    owner, partner = [(jnp.arange(values.shape[axis_at]) // (values.shape[axis_at] // blocks)).reshape([-1 if axis == axis_at else 1 for axis in range(values.ndim)]) for axis_at in (source, target)]
    chosen = jax.random.permutation(rng, blocks)[partner]
    strong = (owner == chosen) | (owner == (partner + blocks // 2) % blocks)
    return jnp.where(strong, factor * values, values)


def steps_of(key, dims, shards, smallest, largest):
    factor_of, own = 1.0, jax.random.fold_in(key, 6)
    for position, parts in shards:
        steps = jnp.exp(jax.random.uniform(jax.random.fold_in(own, position), (parts,), jnp.float32, smallest / len(shards), largest / len(shards)))
        factor_of = factor_of * jnp.repeat(steps, dims[position] // parts).reshape([-1 if axis == position else 1 for axis in range(len(dims))])
    return factor_of


def bell_draw(stream_key, shape, width, limit, cuts=(), kind=jnp.bfloat16):
    array = width * jax.random.normal(stream_key, shape, jnp.float32)
    if cuts:
        array = array * steps_of(stream_key, shape, cuts, -0.22, 0.18)
    return jnp.clip(array, -limit, limit).astype(kind)


def bell_draw_with(key, extent, spread, reach, cuts, heavy, kind=jnp.bfloat16):
    values = spread * jax.random.normal(key, extent, jnp.float32)
    if cuts:
        values = values * steps_of(key, extent, cuts, -0.22, 0.18)
    return jnp.clip(strengthened(values, jax.random.fold_in(key, 3), *heavy), -reach, reach).astype(kind)


def setup_inputs(seed: int = 0) -> dict:
    keys = jax.random.split(jax.random.key(seed), 22)
    inputs = bell_draw_with(keys[0], (TOKENS, D), 1.0, 6.0, ((0, 32),), (0, 1, 32, 2.75))
    cotangent = bell_draw_with(keys[1], (TOKENS, D), 1.0, 6.0, ((0, 32),), (0, 1, 32, 2.75))
    mix_gain = jnp.clip(1.0 + 0.15 * jax.random.normal(keys[2], (D,), jnp.float32), 0.25, 1.75).astype(jnp.bfloat16)
    query_weight = bell_draw(keys[3], (D, HEADS * HEAD_DIM), D ** -0.5, 0.1875, ((0, 8), (1, 4)))
    key_weight = bell_draw(keys[4], (D, KV_HEADS * HEAD_DIM), D ** -0.5, 0.1875, ((0, 8),))
    value_weight = bell_draw(keys[5], (D, KV_HEADS * HEAD_DIM), D ** -0.5, 0.1875, ((0, 8),))
    attention_out = bell_draw(keys[6], (D, HEADS * HEAD_DIM), (max(1, HEADS * HEAD_DIM * 4 // LEN)) ** -0.5, 3.0, ((0, 8), (1, 4)))
    mamba_gate = bell_draw(keys[7], (D, SSM_HEADS * SSM_HEAD_DIM), D ** -0.5, 0.1875, ((0, 8), (1, 4)))
    mamba_input = bell_draw(keys[8], (D, SSM_HEADS * SSM_HEAD_DIM), D ** -0.5, 0.1875, ((0, 8), (1, 4)))
    state_weight = bell_draw(keys[9], (D, 2 * STATE), D ** -0.5, 0.1875, ((0, 8),))
    step_weight = bell_draw(keys[10], (D, SSM_HEADS), D ** -0.5, 0.1875, ((0, 8), (1, 4)))
    mamba_out = bell_draw(keys[11], (D, SSM_HEADS * SSM_HEAD_DIM), (SSM_HEADS * SSM_HEAD_DIM // 4) ** -0.5, 0.3125, ((0, 8), (1, 4)))
    kernel_weight = bell_draw(keys[12], (KCONV, SSM_HEADS * SSM_HEAD_DIM + 2 * STATE), 0.5, 3.0, (), jnp.float32)
    kernel_bias = bell_draw(keys[13], (SSM_HEADS * SSM_HEAD_DIM + 2 * STATE,), 0.5, 3.0, (), jnp.float32)
    decay_log = jnp.clip(jax.random.uniform(keys[14], (SSM_HEADS,), jnp.float32, 0.0, 2.77), 0.0, 2.77)
    step_bias = jnp.clip(jax.random.uniform(keys[15], (SSM_HEADS,), jnp.float32, -4.5, -2.0), -4.5, -2.0)
    skip_weight = jnp.clip(jax.random.uniform(keys[16], (SSM_HEADS,), jnp.float32, 0.5, 2.0), 0.5, 2.0)
    mlp_gain = jnp.clip(1.0 + 0.15 * jax.random.normal(keys[17], (D,), jnp.float32), 0.25, 1.75).astype(jnp.bfloat16)
    gate_weight = bell_draw(keys[18], (D, FF), D ** -0.5, 0.1875, ((0, 8), (1, 4)))
    up_weight = bell_draw(keys[19], (D, FF), D ** -0.5, 0.1875, ((0, 8), (1, 4)))
    down_weight = bell_draw(keys[20], (D, FF), (FF // 2) ** -0.5, 0.1875, ((0, 8), (1, 4)))
    return {"inputs": inputs, "cotangent": cotangent, "mix_gain": mix_gain, "query_weight": query_weight, "key_weight": key_weight, "value_weight": value_weight, "attention_out": attention_out, "mamba_gate": mamba_gate, "mamba_input": mamba_input, "state_weight": state_weight, "step_weight": step_weight, "mamba_out": mamba_out, "kernel_weight": kernel_weight, "kernel_bias": kernel_bias, "decay_log": decay_log, "step_bias": step_bias, "skip_weight": skip_weight, "mlp_gain": mlp_gain, "gate_weight": gate_weight, "up_weight": up_weight, "down_weight": down_weight}


eps = 1e-05
rope_base = 100000000000.0
highest = lax.Precision.HIGHEST

@jax.custom_vjp
def low(v):
    return lax.optimization_barrier(v.astype(jnp.bfloat16)).astype(jnp.float32)

@jax.custom_vjp
def low_back(v):
    return v

def low_keep(v):
    return (low(v), None)

def low_pass(kept, grad):
    return (grad,)

def back_keep(v):
    return (v, None)

def back_low(kept, grad):
    return (low(grad),)
low.defvjp(low_keep, low_pass)
low_back.defvjp(back_keep, back_low)

def rms_norm(values, gain_vector):
    return values * lax.rsqrt(lax.optimization_barrier(jnp.mean(values * values, -1, keepdims=True)) + eps) * gain_vector

def rotary_tables(length):
    half_dim = HEAD_DIM // 2
    frequency = jnp.exp(jnp.arange(half_dim, dtype=jnp.float32) * (-2.0 * math.log(rope_base) / HEAD_DIM))
    angles = jnp.arange(length, dtype=jnp.float32)[:, None] * frequency[None, :]
    return (jnp.cos(angles)[:, None, :], jnp.sin(angles)[:, None, :])

def rotary(values, cosine_table, sine_table):
    half_dim = values.shape[-1] // 2
    former = values[..., :half_dim]
    latter = values[..., half_dim:]
    return jnp.concatenate([former * cosine_table - latter * sine_table, latter * cosine_table + former * sine_table], -1)

def causal_conv(signal, kernel, offset):
    length = signal.shape[0]
    tap_count = kernel.shape[0]
    padded = jnp.concatenate([jnp.zeros((tap_count - 1,) + signal.shape[1:], signal.dtype), signal], 0)
    result = offset
    for lag_index in range(tap_count):
        result = result + kernel[lag_index] * padded[lag_index:lag_index + length]
    return result

def ssd_scan(series, step_sizes, decay_rates, input_map, output_map, skip_gain):
    length, group_count, head_count, head_width = series.shape
    blocks = length // SCAN_BLOCK

    def by_block(values):
        return values.reshape((blocks, SCAN_BLOCK) + values.shape[1:])

    def advance(carry_state, block_data):
        series_block, step_block, input_block, output_block = block_data
        cumulative = jnp.cumsum(step_block * decay_rates, axis=0)
        row_index = lax.broadcasted_iota(jnp.int32, (SCAN_BLOCK, SCAN_BLOCK), 0)
        earlier = lax.broadcasted_iota(jnp.int32, (SCAN_BLOCK, SCAN_BLOCK), 1)
        causal = (row_index >= earlier)[:, :, None, None]
        log_gaps = jnp.where(causal, cumulative[:, None] - cumulative[None, :], -1e+30)
        affinity = jnp.einsum('tgn,sgn->tsg', output_block, input_block, precision=highest)
        weights = jnp.exp(log_gaps) * affinity[..., None]
        scaled = series_block * step_block[..., None]
        within = jnp.einsum('tsgj,sgjp->tgjp', weights, scaled, precision=highest)
        carried = jnp.einsum('tgn,gjpn->tgjp', output_block, carry_state, precision=highest) * jnp.exp(cumulative)[..., None]
        remain = jnp.exp(cumulative[-1][None] - cumulative)
        written = jnp.einsum('sgjp,sgn->gjpn', scaled * remain[..., None], input_block, precision=highest)
        carry_state = carry_state * jnp.exp(cumulative[-1])[..., None, None] + written
        return (carry_state, within + carried + series_block * skip_gain[..., None])
    initial = jnp.zeros((group_count, head_count, head_width, input_map.shape[-1]), jnp.float32)
    _, outputs = lax.scan(advance, initial, (by_block(series), by_block(step_sizes), by_block(input_map), by_block(output_map)))
    return outputs.reshape(series.shape)

def sequence_layer(params, sequence):
    mix_gain, query_weight, key_weight, value_weight, attention_out, mamba_gate, mamba_input, state_weight, step_weight, mamba_out, kernel_weight, kernel_bias, decay_log, step_bias, skip_weight, mlp_gain, gate_weight, up_weight, down_weight = params
    length = sequence.shape[0]
    group_heads = HEADS // N_TENSOR
    normed = low(rms_norm(sequence, mix_gain))
    query_proj = jnp.dot(normed, query_weight, precision=highest).reshape(length, HEADS, HEAD_DIM)
    key_proj = jnp.dot(normed, key_weight, precision=highest).reshape(length, KV_HEADS, HEAD_DIM)
    value_proj = jnp.dot(normed, value_weight, precision=highest).reshape(length, KV_HEADS, HEAD_DIM)
    key_group = jnp.arange(N_TENSOR, dtype=jnp.int32) * group_heads // (HEADS // KV_HEADS)
    head_group = jnp.arange(HEADS, dtype=jnp.int32) // group_heads
    cosine_table, sine_table = rotary_tables(length)
    query_rot = low(rotary(low_back(query_proj), cosine_table, sine_table))
    key_rot = low(rotary(low_back(key_proj[:, key_group]), cosine_table, sine_table))
    value_low = low(low_back(value_proj[:, key_group]))
    raw_scores = low_back(jnp.einsum('qhd,khd->hqk', query_rot, key_rot[:, head_group], precision=highest) * HEAD_DIM ** (-0.5))
    row_index = lax.broadcasted_iota(jnp.int32, (length, length), 0)
    column_index = lax.broadcasted_iota(jnp.int32, (length, length), 1)
    scores = jnp.where((column_index <= row_index)[None], raw_scores, -1e+30)
    weights_low = low(jax.nn.softmax(scores, axis=-1))
    attended = jnp.einsum('hqk,khd->qhd', weights_low, value_low[:, head_group], precision=highest)
    attended = low(low_back(attended.reshape(length, HEADS * HEAD_DIM)))
    attention_branch = jnp.dot(attended, attention_out.T, precision=highest)
    full_width = SSM_HEADS * SSM_HEAD_DIM
    group_width = full_width // N_TENSOR
    scan_heads = SSM_HEADS // N_TENSOR
    gate_proj = low_back(jnp.dot(normed, mamba_gate, precision=highest))
    input_proj = low_back(jnp.dot(normed, mamba_input, precision=highest))
    step_proj = low_back(jnp.dot(normed, step_weight, precision=highest))
    state_proj = jnp.dot(normed, state_weight, precision=highest)
    state_copies = low_back(jnp.broadcast_to(state_proj[:, None], (length, N_TENSOR, 2 * STATE)))
    signal = jnp.concatenate([input_proj.reshape(length, N_TENSOR, group_width), state_copies], 2)
    kernel_group = jnp.concatenate([kernel_weight[:, :full_width].reshape(KCONV, N_TENSOR, group_width), jnp.broadcast_to(kernel_weight[:, None, full_width:], (KCONV, N_TENSOR, 2 * STATE))], 2)
    bias_group = jnp.concatenate([kernel_bias[:full_width].reshape(N_TENSOR, group_width), jnp.broadcast_to(kernel_bias[None, full_width:], (N_TENSOR, 2 * STATE))], 1)
    activated = jax.nn.silu(causal_conv(signal, kernel_group, bias_group))
    series = activated[:, :, :group_width].reshape(length, N_TENSOR, scan_heads, SSM_HEAD_DIM)
    input_map = activated[:, :, group_width:group_width + STATE]
    output_map = activated[:, :, group_width + STATE:]
    step_sizes = jax.nn.softplus(step_proj + step_bias).reshape(length, N_TENSOR, scan_heads)
    decay_rates = (-jnp.exp(decay_log)).reshape(N_TENSOR, scan_heads)
    scanned = ssd_scan(series, step_sizes, decay_rates, input_map, output_map, skip_weight.reshape(N_TENSOR, scan_heads))
    gated_out = low(scanned.reshape(length, full_width) * jax.nn.silu(gate_proj))
    mamba_branch = jnp.dot(gated_out, mamba_out.T, precision=highest)
    hidden = sequence + low_back(attention_branch + mamba_branch)
    normed_mlp = low(rms_norm(hidden, mlp_gain))
    gate_pre = low_back(jnp.dot(normed_mlp, gate_weight, precision=highest))
    up_pre = low_back(jnp.dot(normed_mlp, up_weight, precision=highest))
    hidden_units = low(jax.nn.silu(gate_pre) * up_pre)
    return hidden + jnp.dot(hidden_units, down_weight.T, precision=highest)

def reference(inputs, cotangent, mix_gain, query_weight, key_weight, value_weight, attention_out, mamba_gate, mamba_input, state_weight, step_weight, mamba_out, kernel_weight, kernel_bias, decay_log, step_bias, skip_weight, mlp_gain, gate_weight, up_weight, down_weight):
    params = tuple((weight.astype(jnp.float32) for weight in (mix_gain, query_weight, key_weight, value_weight, attention_out, mamba_gate, mamba_input, state_weight, step_weight, mamba_out, kernel_weight, kernel_bias, decay_log, step_bias, skip_weight, mlp_gain, gate_weight, up_weight, down_weight)))

    def layer(values, flat_rows):
        sequences = flat_rows.reshape(-1, LEN, D)

        def single(sequence):
            return sequence_layer(values, sequence)
        return lax.map(jax.checkpoint(single), sequences).reshape(flat_rows.shape)
    result, backward = jax.vjp(layer, params, inputs.astype(jnp.float32))
    grad_params, grad_inputs = backward(cotangent.astype(jnp.float32))
    return (result.astype(jnp.bfloat16), grad_inputs.astype(jnp.bfloat16), grad_params[0], grad_params[1], grad_params[2], grad_params[3], grad_params[4], grad_params[5], grad_params[6], grad_params[7], grad_params[8], grad_params[9], grad_params[10], grad_params[11], grad_params[12], grad_params[13], grad_params[14], grad_params[15], grad_params[16], grad_params[17], grad_params[18])
```

```python
import math

import jax
import jax.numpy as jnp
from jax import lax
from jax.sharding import PartitionSpec as P

D = 1024
HEADS = 8
KV_HEADS = 2
HEAD_DIM = 64
SSM_HEADS = 24
SSM_HEAD_DIM = 64
STATE = 128
KCONV = 4
SCAN_BLOCK = 128


eps = 1e-05
rope_base = 100000000000.0
highest = lax.Precision.HIGHEST
by_rows = (((0,), (0,)), ((), ()))
by_columns = (((1,), (1,)), ((), ()))


def rms_norm(values, gain_vector):
    return values * lax.rsqrt(jnp.mean(values * values, -1, keepdims=True) + eps) * gain_vector


def rotary_tables(length):
    half_dim = HEAD_DIM // 2
    frequency = jnp.exp(
        jnp.arange(half_dim, dtype=jnp.float32) * (-2.0 * math.log(rope_base) / HEAD_DIM)
    )
    angles = jnp.arange(length, dtype=jnp.float32)[:, None] * frequency[None, :]
    return (jnp.cos(angles)[:, None, :], jnp.sin(angles)[:, None, :])


def rotary(values, cosine_table, sine_table):
    half_dim = values.shape[-1] // 2
    former = values[..., :half_dim]
    latter = values[..., half_dim:]
    return jnp.concatenate(
        [former * cosine_table - latter * sine_table, latter * cosine_table + former * sine_table],
        -1,
    )


def unrotate(gradient, cosine_table, sine_table):
    half_dim = gradient.shape[-1] // 2
    former = gradient[..., :half_dim]
    latter = gradient[..., half_dim:]
    return jnp.concatenate(
        [former * cosine_table + latter * sine_table, latter * cosine_table - former * sine_table],
        -1,
    )


def causal_conv(signal, kernel, offset):
    length = signal.shape[0]
    tap_count = kernel.shape[0]
    padded = jnp.concatenate(
        [jnp.zeros((tap_count - 1,) + signal.shape[1:], signal.dtype), signal], 0
    )
    result = offset
    for lag_index in range(tap_count):
        result = result + kernel[lag_index] * padded[lag_index : lag_index + length]
    return result


def ssd_scan(series, step_sizes, decay_rates, input_map, output_map, skip_gain):
    length, group_count, head_count, head_width = series.shape
    blocks = length // SCAN_BLOCK

    def by_block(values):
        return values.reshape((blocks, SCAN_BLOCK) + values.shape[1:])

    def advance(carry_state, block_data):
        series_block, step_block, input_block, output_block = block_data
        cumulative = jnp.cumsum(step_block * decay_rates, axis=0)
        row_index = lax.broadcasted_iota(jnp.int32, (SCAN_BLOCK, SCAN_BLOCK), 0)
        earlier = lax.broadcasted_iota(jnp.int32, (SCAN_BLOCK, SCAN_BLOCK), 1)
        causal = (row_index >= earlier)[:, :, None, None]
        log_gaps = jnp.where(causal, cumulative[:, None] - cumulative[None, :], -1e30)
        affinity = jnp.einsum("tgn,sgn->tsg", output_block, input_block, precision=highest)
        weights = jnp.exp(log_gaps) * affinity[..., None]
        scaled = series_block * step_block[..., None]
        within = jnp.einsum("tsgj,sgjp->tgjp", weights, scaled, precision=highest)
        carried = (
            jnp.einsum("tgn,gjpn->tgjp", output_block, carry_state, precision=highest)
            * jnp.exp(cumulative)[..., None]
        )
        remain = jnp.exp(cumulative[-1][None] - cumulative)
        written = jnp.einsum(
            "sgjp,sgn->gjpn", scaled * remain[..., None], input_block, precision=highest
        )
        carry_state = carry_state * jnp.exp(cumulative[-1])[..., None, None] + written
        return (carry_state, within + carried + series_block * skip_gain[..., None])

    initial = jnp.zeros((group_count, head_count, head_width, input_map.shape[-1]), jnp.float32)
    _, outputs = lax.scan(
        advance,
        initial,
        (by_block(series), by_block(step_sizes), by_block(input_map), by_block(output_map)),
    )
    return outputs.reshape(series.shape)


def mamba_core(
    gate_proj,
    input_proj,
    state_proj,
    step_proj,
    kernel_local,
    bias_local,
    decay_local,
    step_local,
    skip_local,
):
    length, channel_count = input_proj.shape
    heads_here = step_proj.shape[1]
    activated = jax.nn.silu(
        causal_conv(jnp.concatenate([input_proj, state_proj], 1), kernel_local, bias_local)
    )
    series = activated[:, :channel_count].reshape(
        length, 1, heads_here, channel_count // heads_here
    )
    input_map = activated[:, channel_count : channel_count + STATE][:, None]
    output_map = activated[:, channel_count + STATE :][:, None]
    step_sizes = jax.nn.softplus(step_proj + step_local)[:, None]
    decay_rates = (-jnp.exp(decay_local))[None]
    scanned = ssd_scan(series, step_sizes, decay_rates, input_map, output_map, skip_local[None])
    return scanned.reshape(length, channel_count) * jax.nn.silu(gate_proj)


def partner_pairs(count):
    return [(index, index ^ 1) for index in range(count)]


def shift_pairs(count, steps):
    return [(index, (index + 2 * steps) % count) for index in range(count)]


def gather_dp(piece):
    count = lax.axis_size("dp")
    if count > 8 or count % 2:
        return lax.all_gather(piece, "dp", axis=0, tiled=True)
    mine = lax.axis_index("dp")
    rows = piece.shape[0]
    result = jnp.zeros((count * rows,) + piece.shape[1:], piece.dtype)

    def put(result, block, source):
        return lax.dynamic_update_slice_in_dim(result, block, source * rows, 0)

    far = [lax.ppermute(piece, "dp", shift_pairs(count, steps)) for steps in range(1, count // 2)]
    near = lax.ppermute(piece, "dp", partner_pairs(count))
    crossed = [lax.ppermute(block, "dp", partner_pairs(count)) for block in far]
    other = mine + 1 - 2 * (mine % 2)
    result = put(result, piece, mine)
    result = put(result, near, other)
    for steps in range(1, count // 2):
        result = put(result, far[steps - 1], (mine - 2 * steps + count) % count)
        result = put(result, crossed[steps - 1], (other - 2 * steps + count) % count)
    return result


def reduce_dp(partial):
    count = lax.axis_size("dp")
    rows = partial.shape[0] // count
    if count > 8 or count % 2:
        return lax.psum_scatter(partial, "dp", scatter_dimension=0, tiled=True).astype(jnp.float32)
    mine = lax.axis_index("dp")
    side = mine % 2
    place = mine // 2
    half_count = count // 2
    split = partial.reshape((half_count, 2, rows) + partial.shape[1:])
    sent = lax.dynamic_index_in_dim(split, 1 - side, 1, keepdims=False)
    kept = lax.dynamic_index_in_dim(split, side, 1, keepdims=False)
    arrived = lax.ppermute(sent, "dp", partner_pairs(count))
    paired = (kept.astype(jnp.float32) + arrived.astype(jnp.float32)).astype(jnp.bfloat16)
    total = lax.dynamic_index_in_dim(paired, place, 0, keepdims=False).astype(jnp.float32)
    for steps in range(1, half_count):
        block = lax.dynamic_index_in_dim(paired, (place + steps) % half_count, 0, keepdims=False)
        total = total + lax.ppermute(block, "dp", shift_pairs(count, steps)).astype(jnp.float32)
    return total


def full_rows(local_piece):
    return lax.all_gather(local_piece, "tensor", axis=0, tiled=True)


def summed_rows(operand_pairs, row_count):
    running = jnp.zeros(
        (row_count * lax.axis_size("tensor"), operand_pairs[0][1].shape[0]), jnp.float32
    )
    for left_side, right_side in operand_pairs:
        running = running + lax.dot_general(
            left_side, right_side, by_columns, preferred_element_type=jnp.float32
        )
    return lax.psum_scatter(
        running.astype(jnp.bfloat16), "tensor", scatter_dimension=0, tiled=True
    ).astype(jnp.float32)


def weight_grad(activations, gradient):
    return lax.dot_general(activations, gradient, by_rows, preferred_element_type=jnp.float32)


def block_scores(query_block, key_rot, first_row, score_scale):
    raw_scores = (
        jnp.einsum("qhd,kd->hqk", query_block, key_rot, preferred_element_type=jnp.float32)
        * score_scale
    )
    row_index = first_row + lax.broadcasted_iota(jnp.int32, raw_scores.shape, 1)
    column_index = lax.broadcasted_iota(jnp.int32, raw_scores.shape, 2)
    return jnp.where(column_index <= row_index, raw_scores, -1e30)


def local(
    inputs,
    cotangent,
    mix_gain,
    query_weight,
    key_weight,
    value_weight,
    attention_out,
    mamba_gate,
    mamba_input,
    state_weight,
    step_weight,
    mamba_out,
    kernel_weight,
    kernel_bias,
    decay_log,
    step_bias,
    skip_weight,
    mlp_gain,
    gate_weight,
    up_weight,
    down_weight,
):
    tensor_index = lax.axis_index("tensor")
    local_rows = inputs.shape[0]
    query_heads = query_weight.shape[1] // HEAD_DIM
    key_head = tensor_index * query_heads // (HEADS // KV_HEADS)
    unit_count = gate_weight.shape[1]
    scan_width = mamba_input.shape[1]
    scan_heads = step_weight.shape[1]
    weight_rows = query_weight.shape[0]
    narrow = jnp.concatenate(
        [
            step_weight,
            mix_gain[:, None],
            mlp_gain[:, None],
            jnp.zeros((weight_rows, 128 - scan_heads - 2), jnp.bfloat16),
        ],
        1,
    )
    key_own = lax.dynamic_slice_in_dim(key_weight, key_head * HEAD_DIM, HEAD_DIM, 1)
    value_own = lax.dynamic_slice_in_dim(value_weight, key_head * HEAD_DIM, HEAD_DIM, 1)
    mix_pack = gather_dp(
        jnp.concatenate(
            [mamba_gate, mamba_input, state_weight, query_weight, key_own, value_own, narrow], 1
        )
    )
    out_pack = gather_dp(jnp.concatenate([attention_out, mamba_out], 1))
    mlp_pack = gather_dp(jnp.concatenate([gate_weight, up_weight, down_weight], 1))

    def take(pack, widths):
        pieces, start = [], 0
        for width in widths:
            pieces.append(pack[:, start : start + width])
            start += width
        return pieces

    query_width = query_weight.shape[1]
    gate_ssm_all, input_ssm_all, state_all, query_all, key_slice, value_slice, narrow_all = take(
        mix_pack,
        (scan_width, scan_width, state_weight.shape[1], query_width, HEAD_DIM, HEAD_DIM, 128),
    )
    step_all = narrow_all[:, :scan_heads]
    mix_gain_all = narrow_all[:, scan_heads]
    mlp_gain_all = narrow_all[:, scan_heads + 1]
    attention_all, mamba_out_all = take(out_pack, (query_width, scan_width))
    gate_all, up_all, down_all = take(mlp_pack, (unit_count,) * 3)
    full_width = SSM_HEADS * SSM_HEAD_DIM
    kernel_local = jnp.concatenate(
        [
            lax.dynamic_slice_in_dim(kernel_weight, tensor_index * scan_width, scan_width, 1),
            kernel_weight[:, full_width:],
        ],
        1,
    )
    bias_local = jnp.concatenate(
        [
            lax.dynamic_slice_in_dim(kernel_bias, tensor_index * scan_width, scan_width, 0),
            kernel_bias[full_width:],
        ],
        0,
    )
    decay_local = lax.dynamic_slice_in_dim(decay_log, tensor_index * scan_heads, scan_heads, 0)
    step_local = lax.dynamic_slice_in_dim(step_bias, tensor_index * scan_heads, scan_heads, 0)
    skip_local = lax.dynamic_slice_in_dim(skip_weight, tensor_index * scan_heads, scan_heads, 0)
    rows_float = inputs.astype(jnp.float32)
    normed, first_norm_back = jax.vjp(rms_norm, rows_float, mix_gain_all.astype(jnp.float32))
    normed_local = normed.astype(jnp.bfloat16)
    mixer_rows = full_rows(normed_local)
    length = mixer_rows.shape[0]
    cosine_table, sine_table = rotary_tables(length)
    query_proj = jnp.dot(mixer_rows, query_all, preferred_element_type=jnp.float32).reshape(
        length, query_heads, HEAD_DIM
    )
    key_proj = jnp.dot(mixer_rows, key_slice, preferred_element_type=jnp.float32)
    value_proj = jnp.dot(mixer_rows, value_slice, preferred_element_type=jnp.float32)
    query_rot = rotary(query_proj, cosine_table, sine_table).astype(jnp.bfloat16)
    key_rot = rotary(key_proj[:, None], cosine_table, sine_table)[:, 0].astype(jnp.bfloat16)
    value_low = value_proj.astype(jnp.bfloat16)
    block_rows = min(512, length)
    block_count = length // block_rows
    score_scale = HEAD_DIM ** (-0.5)
    block_ids = jnp.arange(block_count, dtype=jnp.int32)

    def attend_block(block_index):
        first_row = block_index * block_rows
        scores = block_scores(query_rot, key_rot, first_row, score_scale)
        row_max = jnp.max(scores, -1, keepdims=True)
        shifted = jnp.exp(scores - row_max)
        row_total = jnp.sum(shifted, -1, keepdims=True)
        weights_low = (shifted / row_total).astype(jnp.bfloat16)
        attended = jnp.einsum(
            "hqk,kd->qhd", weights_low, value_low, preferred_element_type=jnp.float32
        )
        return (attended, (row_max + jnp.log(row_total))[..., 0])

    attended_blocks, log_totals = lax.map(attend_block, block_ids)
    attended_low = attended_blocks.reshape(length, query_heads * HEAD_DIM).astype(jnp.bfloat16)
    gate_proj = jnp.dot(mixer_rows, gate_ssm_all, preferred_element_type=jnp.float32)
    input_proj = jnp.dot(mixer_rows, input_ssm_all, preferred_element_type=jnp.float32)
    state_proj = jnp.dot(mixer_rows, state_all, preferred_element_type=jnp.float32)
    step_proj = jnp.dot(mixer_rows, step_all, preferred_element_type=jnp.float32)
    gated_out, mamba_back = jax.vjp(
        mamba_core,
        gate_proj,
        input_proj,
        state_proj,
        step_proj,
        kernel_local,
        bias_local,
        decay_local,
        step_local,
        skip_local,
    )
    gated_low = gated_out.astype(jnp.bfloat16)
    mixed = summed_rows(((attended_low, attention_all), (gated_low, mamba_out_all)), local_rows)
    hidden = rows_float + mixed
    normed_mlp, second_norm_back = jax.vjp(rms_norm, hidden, mlp_gain_all.astype(jnp.float32))
    normed_mlp_local = normed_mlp.astype(jnp.bfloat16)
    mlp_rows = full_rows(normed_mlp_local)
    gate_pre = jnp.dot(mlp_rows, gate_all, preferred_element_type=jnp.float32)
    up_pre = jnp.dot(mlp_rows, up_all, preferred_element_type=jnp.float32)
    sigmoid_gate = jax.nn.sigmoid(gate_pre)
    silu_gate = gate_pre * sigmoid_gate
    units_low = (silu_gate * up_pre).astype(jnp.bfloat16)
    mlp_sum = summed_rows(((units_low, down_all),), local_rows)
    output = (hidden + mlp_sum).astype(jnp.bfloat16)
    cotangent_rows = full_rows(cotangent)
    grad_down = weight_grad(cotangent_rows, units_low)
    unit_grad = jnp.dot(cotangent_rows, down_all, preferred_element_type=jnp.float32)
    gate_grad = (
        unit_grad * up_pre * (sigmoid_gate * (1.0 + gate_pre * (1.0 - sigmoid_gate)))
    ).astype(jnp.bfloat16)
    up_grad = (unit_grad * silu_gate).astype(jnp.bfloat16)
    grad_gate = weight_grad(mlp_rows, gate_grad)
    grad_up = weight_grad(mlp_rows, up_grad)
    mlp_input_grad = summed_rows(((gate_grad, gate_all), (up_grad, up_all)), local_rows)
    hidden_norm_grad, grad_mlp_gain = second_norm_back(mlp_input_grad)
    hidden_grad = cotangent.astype(jnp.float32) + hidden_norm_grad
    mixer_grad_rows = full_rows(hidden_grad.astype(jnp.bfloat16))
    grad_attention = weight_grad(mixer_grad_rows, attended_low)
    grad_mamba_out = weight_grad(mixer_grad_rows, gated_low)
    attended_grad = (
        jnp.dot(mixer_grad_rows, attention_all, preferred_element_type=jnp.float32)
        .astype(jnp.bfloat16)
        .reshape(length, query_heads, HEAD_DIM)
    )
    gated_grad = jnp.dot(mixer_grad_rows, mamba_out_all, preferred_element_type=jnp.float32)

    def attend_back(carried, block_index):
        key_total, value_total = carried
        first_row = block_index * block_rows
        scores = block_scores(query_rot, key_rot, first_row, score_scale)
        probabilities = jnp.exp(scores - log_totals[block_index][..., None])
        prob_grad = jnp.einsum(
            "qhd,kd->hqk", attended_grad, value_low, preferred_element_type=jnp.float32
        )
        row_dot = jnp.sum(prob_grad * probabilities, -1, keepdims=True)
        score_grad = (probabilities * (prob_grad - row_dot)).astype(jnp.bfloat16)
        query_grad = (
            jnp.einsum("hqk,kd->qhd", score_grad, key_rot, preferred_element_type=jnp.float32)
            * score_scale
        )
        key_total = (
            key_total
            + jnp.einsum("hqk,qhd->kd", score_grad, query_rot, preferred_element_type=jnp.float32)
            * score_scale
        )
        value_total = value_total + jnp.einsum(
            "hqk,qhd->kd",
            probabilities.astype(jnp.bfloat16),
            attended_grad,
            preferred_element_type=jnp.float32,
        )
        return ((key_total, value_total), query_grad)

    zero_keys = jnp.zeros((length, HEAD_DIM), jnp.float32)
    (key_total, value_total), query_grads = lax.scan(attend_back, (zero_keys, zero_keys), block_ids)
    query_low = (
        unrotate(query_grads.reshape(length, query_heads, HEAD_DIM), cosine_table, sine_table)
        .astype(jnp.bfloat16)
        .reshape(length, query_heads * HEAD_DIM)
    )
    key_low = unrotate(key_total[:, None], cosine_table, sine_table)[:, 0].astype(jnp.bfloat16)
    value_grad_low = value_total.astype(jnp.bfloat16)
    (
        gate_proj_grad,
        input_proj_grad,
        state_proj_grad,
        step_proj_grad,
        kernel_grad,
        bias_grad,
        decay_grad,
        step_bias_grad,
        skip_grad,
    ) = mamba_back(gated_grad)
    gate_proj_low = gate_proj_grad.astype(jnp.bfloat16)
    input_proj_low = input_proj_grad.astype(jnp.bfloat16)
    state_proj_low = state_proj_grad.astype(jnp.bfloat16)
    step_proj_low = step_proj_grad.astype(jnp.bfloat16)
    mixer_input_grad = summed_rows(
        (
            (query_low, query_all),
            (key_low, key_slice),
            (value_grad_low, value_slice),
            (gate_proj_low, gate_ssm_all),
            (input_proj_low, input_ssm_all),
            (state_proj_low, state_all),
            (step_proj_low, step_all),
        ),
        local_rows,
    )
    input_norm_grad, grad_mix_gain = first_norm_back(mixer_input_grad)
    grad_inputs = (hidden_grad + input_norm_grad).astype(jnp.bfloat16)
    grad_query = weight_grad(mixer_rows, query_low)
    key_width = key_weight.shape[1]
    grad_key = lax.dynamic_update_slice_in_dim(
        jnp.zeros((D, key_width), jnp.float32),
        weight_grad(mixer_rows, key_low),
        key_head * HEAD_DIM,
        1,
    )
    grad_value = lax.dynamic_update_slice_in_dim(
        jnp.zeros((D, key_width), jnp.float32),
        weight_grad(mixer_rows, value_grad_low),
        key_head * HEAD_DIM,
        1,
    )
    grad_gate_ssm = weight_grad(mixer_rows, gate_proj_low)
    grad_input_ssm = weight_grad(mixer_rows, input_proj_low)
    grad_state = weight_grad(mixer_rows, state_proj_low)
    grad_step = weight_grad(mixer_rows, step_proj_low)
    kernel_full = jnp.concatenate(
        [
            lax.dynamic_update_slice_in_dim(
                jnp.zeros((KCONV, full_width), jnp.float32),
                kernel_grad[:, :scan_width],
                tensor_index * scan_width,
                1,
            ),
            kernel_grad[:, scan_width:],
        ],
        1,
    )
    bias_full = jnp.concatenate(
        [
            lax.dynamic_update_slice_in_dim(
                jnp.zeros((full_width,), jnp.float32),
                bias_grad[:scan_width],
                tensor_index * scan_width,
                0,
            ),
            bias_grad[scan_width:],
        ],
        0,
    )
    decay_full = lax.dynamic_update_slice_in_dim(
        jnp.zeros((SSM_HEADS,), jnp.float32), decay_grad, tensor_index * scan_heads, 0
    )
    step_bias_full = lax.dynamic_update_slice_in_dim(
        jnp.zeros((SSM_HEADS,), jnp.float32), step_bias_grad, tensor_index * scan_heads, 0
    )
    skip_full = lax.dynamic_update_slice_in_dim(
        jnp.zeros((SSM_HEADS,), jnp.float32), skip_grad, tensor_index * scan_heads, 0
    )
    count = lax.axis_size("dp")
    tensor_size = lax.axis_size("tensor")
    low = jnp.bfloat16
    shared = jnp.concatenate(
        [
            grad_key,
            grad_value,
            grad_state,
            grad_mix_gain[:, None],
            grad_mlp_gain[:, None],
            jnp.zeros((D, 126), jnp.float32),
        ],
        1,
    ).astype(low)
    shared_width = shared.shape[1]
    shared = lax.psum_scatter(
        shared.reshape(count, tensor_size, D // count // tensor_size, shared_width),
        "tensor",
        scatter_dimension=1,
        tiled=True,
    )
    shared = shared.reshape(D, shared_width // tensor_size)
    mlp_sum_pack = reduce_dp(jnp.concatenate([grad_gate, grad_up, grad_down], 1).astype(low))
    out_sum_pack = reduce_dp(jnp.concatenate([grad_attention, grad_mamba_out], 1).astype(low))
    mix_sum_pack = reduce_dp(
        jnp.concatenate(
            [
                grad_gate_ssm.astype(low),
                grad_input_ssm.astype(low),
                grad_query.astype(low),
                shared,
                grad_step.astype(low),
            ],
            1,
        )
    )
    mlp_sums = take(mlp_sum_pack, (unit_count,) * 3)
    attention_sum, mamba_out_sum = take(out_sum_pack, (query_width, scan_width))
    gate_ssm_sum, input_ssm_sum, query_sum, shared_sum, step_sum = take(
        mix_sum_pack,
        (scan_width, scan_width, query_width, shared_width // tensor_size, scan_heads),
    )
    shared_sum = shared_sum.reshape(D // count // tensor_size, shared_width)
    key_sum, value_sum, state_sum = take(
        shared_sum, (key_width, key_width, state_weight.shape[1])
    )
    mix_gain_sum = shared_sum[:, shared_width - 128]
    mlp_gain_sum = shared_sum[:, shared_width - 127]
    mix_sums = (query_sum, attention_sum, gate_ssm_sum, input_ssm_sum, step_sum, mamba_out_sum)
    shared_sums = (mix_gain_sum, mlp_gain_sum, key_sum, value_sum, state_sum)
    small_parts = (kernel_full, bias_full, decay_full, step_bias_full, skip_full)
    small_flat = lax.psum(
        jnp.concatenate([part.reshape(-1) for part in small_parts]), ("dp", "tensor")
    )
    small_sums, start = [], 0
    for part in small_parts:
        small_sums.append(small_flat[start : start + part.size].reshape(part.shape))
        start += part.size
    return (
        output,
        grad_inputs,
        shared_sums[0],
        mix_sums[0],
        shared_sums[2],
        shared_sums[3],
        mix_sums[1],
        mix_sums[2],
        mix_sums[3],
        shared_sums[4],
        mix_sums[4],
        mix_sums[5],
        small_sums[0],
        small_sums[1],
        small_sums[2],
        small_sums[3],
        small_sums[4],
        shared_sums[1],
        mlp_sums[0],
        mlp_sums[1],
        mlp_sums[2],
    )


def solution(mesh):
    placed = (
        P(("dp", "tensor"), None),
        P(("dp", "tensor"), None),
        P("dp"),
        P("dp", "tensor"),
        P("dp", None),
        P("dp", None),
        P("dp", "tensor"),
        P("dp", "tensor"),
        P("dp", "tensor"),
        P("dp", None),
        P("dp", "tensor"),
        P("dp", "tensor"),
        P(),
        P(),
        P(),
        P(),
        P(),
        P("dp"),
        P("dp", "tensor"),
        P("dp", "tensor"),
        P("dp", "tensor"),
    )
    return jax.shard_map(
        local,
        mesh=mesh,
        in_specs=placed,
        out_specs=(
            P(("dp", "tensor"), None),
            P(("dp", "tensor"), None),
            P(("dp", "tensor")),
            P("dp", "tensor"),
            P(("dp", "tensor"), None),
            P(("dp", "tensor"), None),
            P("dp", "tensor"),
            P("dp", "tensor"),
            P("dp", "tensor"),
            P(("dp", "tensor"), None),
            P("dp", "tensor"),
            P("dp", "tensor"),
            P(),
            P(),
            P(),
            P(),
            P(),
            P(("dp", "tensor")),
            P("dp", "tensor"),
            P("dp", "tensor"),
            P("dp", "tensor"),
        ),
        check_vma=False,
    )
```

```python
import functools
import math

import jax
import jax.numpy as jnp
from jax import lax
from jax.experimental import pallas as pl
from jax.experimental.pallas import tpu as pltpu
from jax.sharding import PartitionSpec as P

D = 1024
HEADS = 8
KV_HEADS = 2
HEAD_DIM = 64
SSM_HEADS = 24
SSM_HEAD_DIM = 64
STATE = 128
KCONV = 4
SCAN_BLOCK = 128


eps = 1e-05
rope_base = 100000000000.0
highest = lax.Precision.HIGHEST
by_rows = (((0,), (0,)), ((), ()))
by_columns = (((1,), (1,)), ((), ()))


def rms_norm(values, gain_vector):
    return values * lax.rsqrt(jnp.mean(values * values, -1, keepdims=True) + eps) * gain_vector


def rotary_tables(length):
    half_dim = HEAD_DIM // 2
    frequency = jnp.exp(
        jnp.arange(half_dim, dtype=jnp.float32) * (-2.0 * math.log(rope_base) / HEAD_DIM)
    )
    angles = jnp.arange(length, dtype=jnp.float32)[:, None] * frequency[None, :]
    return (jnp.cos(angles)[:, None, :], jnp.sin(angles)[:, None, :])


def rotary(values, cosine_table, sine_table):
    half_dim = values.shape[-1] // 2
    former = values[..., :half_dim]
    latter = values[..., half_dim:]
    return jnp.concatenate(
        [former * cosine_table - latter * sine_table, latter * cosine_table + former * sine_table],
        -1,
    )


def unrotate(gradient, cosine_table, sine_table):
    half_dim = gradient.shape[-1] // 2
    former = gradient[..., :half_dim]
    latter = gradient[..., half_dim:]
    return jnp.concatenate(
        [former * cosine_table + latter * sine_table, latter * cosine_table - former * sine_table],
        -1,
    )


def causal_conv(signal, kernel, offset):
    length = signal.shape[0]
    tap_count = kernel.shape[0]
    padded = jnp.concatenate(
        [jnp.zeros((tap_count - 1,) + signal.shape[1:], signal.dtype), signal], 0
    )
    result = offset
    for lag_index in range(tap_count):
        result = result + kernel[lag_index] * padded[lag_index : lag_index + length]
    return result


def low_dot(left, right, dims):
    return lax.dot_general(
        left.astype(jnp.bfloat16),
        right.astype(jnp.bfloat16),
        dims,
        preferred_element_type=jnp.float32,
    )


plain = (((1,), (0,)), ((), ()))


def head_lanes(values, first_head, heads, width):
    rows = values.shape[0]
    lane = lax.broadcasted_iota(jnp.int32, (rows, heads * width), 1)
    spread = jnp.broadcast_to(values[:, first_head : first_head + 1], lane.shape)
    for index in range(1, heads):
        column = first_head + index
        spread = jnp.where(
            lane < index * width,
            spread,
            jnp.broadcast_to(values[:, column : column + 1], lane.shape),
        )
    return spread


def decay_weights(column, row):
    size = column.shape[0]
    later = lax.broadcasted_iota(jnp.int32, (size, size), 0)
    earlier = lax.broadcasted_iota(jnp.int32, (size, size), 1)
    return jnp.exp(jnp.where(later >= earlier, column - row, -1e30))


def scan_forward_kernel(
    slab_heads, width, heads, x_ref, cum_ref, cumt_ref, b_ref, c_ref, y_ref, saved_ref, state_ref
):
    @pl.when(pl.program_id(0) == 0)
    def _():
        state_ref[...] = jnp.zeros_like(state_ref)

    size = x_ref.shape[0]
    slab = slab_heads * width
    saved_ref[0] = state_ref[...]
    cum = cum_ref[...]
    input_map, output_map = b_ref[...], c_ref[...]
    affinity = low_dot(output_map, input_map, by_columns)
    lane = lax.broadcasted_iota(jnp.int32, (size, slab), 1)
    for first in range(0, heads, slab_heads):
        cols = slice(first * width, first * width + slab)
        series = x_ref[:, cols]
        state = state_ref[:, cols]
        spread = head_lanes(cum, first, slab_heads, width)
        last = spread[size - 1 : size]
        result = low_dot(output_map, state, plain) * jnp.exp(spread)
        for index in range(slab_heads):
            head = first + index
            decay = decay_weights(cum[:, head : head + 1], cumt_ref[head : head + 1, :])
            own = (lane >= index * width) & (lane < (index + 1) * width)
            result = result + low_dot(decay * affinity, jnp.where(own, series, 0.0), plain)
        y_ref[:, cols] = result
        state_ref[:, cols] = state * jnp.exp(last) + low_dot(
            input_map, series * jnp.exp(last - spread), by_rows
        )


def scan_backward_kernel(
    slab_heads,
    width,
    heads,
    x_ref,
    cum_ref,
    cumt_ref,
    b_ref,
    c_ref,
    saved_ref,
    g_ref,
    dx_ref,
    dcum_ref,
    dcumt_ref,
    db_ref,
    dc_ref,
    state_ref,
):
    @pl.when(pl.program_id(0) == 0)
    def _():
        state_ref[...] = jnp.zeros_like(state_ref)

    size = x_ref.shape[0]
    slab = slab_heads * width
    cum = cum_ref[...]
    input_map, output_map = b_ref[...], c_ref[...]
    affinity = low_dot(output_map, input_map, by_columns)
    lane = lax.broadcasted_iota(jnp.int32, (size, slab), 1)
    cum_lane = lax.broadcasted_iota(jnp.int32, cum.shape, 1)
    cum_row = lax.broadcasted_iota(jnp.int32, cum.shape, 0)
    d_cum = jnp.zeros(cum.shape, jnp.float32)
    d_affinity = jnp.zeros((size, size), jnp.float32)
    d_input = jnp.zeros(input_map.shape, jnp.float32)
    d_output = jnp.zeros(output_map.shape, jnp.float32)
    dcumt_ref[...] = jnp.zeros_like(dcumt_ref)
    for first in range(0, heads, slab_heads):
        cols = slice(first * width, first * width + slab)
        series = x_ref[:, cols]
        gradient = g_ref[:, cols]
        state = saved_ref[0, :, cols]
        d_state = state_ref[:, cols]
        spread = head_lanes(cum, first, slab_heads, width)
        last = spread[size - 1 : size]
        remain = jnp.exp(last - spread)
        grown = gradient * jnp.exp(spread)
        kept = series * remain
        d_kept = low_dot(input_map, d_state, plain)
        d_output = d_output + low_dot(grown, state, by_columns)
        d_input = d_input + low_dot(kept, d_state, by_columns)
        written = d_kept * kept
        position = grown * low_dot(output_map, state, plain) - written
        decayed = d_state * jnp.exp(last)
        final = jnp.sum(decayed * state, 0, keepdims=True) + jnp.sum(written, 0, keepdims=True)
        d_series = d_kept * remain
        for index in range(slab_heads):
            head = first + index
            decay = decay_weights(cum[:, head : head + 1], cumt_ref[head : head + 1, :])
            own = (lane >= index * width) & (lane < (index + 1) * width)
            own_gradient = jnp.where(own, gradient, 0.0)
            d_weights = low_dot(own_gradient, series, by_columns) * decay
            d_affinity = d_affinity + d_weights
            d_gaps = d_weights * affinity
            d_series = d_series + low_dot(decay * affinity, own_gradient, by_rows)
            column = jnp.sum(d_gaps, 1, keepdims=True) + jnp.sum(
                jnp.where(own, position, 0.0), 1, keepdims=True
            )
            total = jnp.sum(jnp.where(own[:1], final, 0.0), 1, keepdims=True)
            column = jnp.where(cum_row == size - 1, column + total, column)
            d_cum = jnp.where(cum_lane == head, column, d_cum)
            dcumt_ref[head : head + 1, :] = -jnp.sum(d_gaps, 0, keepdims=True)
        dx_ref[:, cols] = d_series
        state_ref[:, cols] = decayed + low_dot(output_map, grown, by_rows)
    dcum_ref[...] = d_cum
    db_ref[...] = d_input + low_dot(d_affinity, output_map, by_rows)
    dc_ref[...] = d_output + low_dot(d_affinity, input_map, plain)


def scan_sizes(series, cum):
    length, channels = series.shape
    heads = cum.shape[1]
    width = channels // heads
    slab_heads = max(1, 128 // width)
    while heads % slab_heads:
        slab_heads -= 1
    return length, channels, heads, width, slab_heads, length // SCAN_BLOCK


def padded_cum(cum, heads):
    padded = -(-heads // 8) * 8
    return jnp.pad(cum, ((0, 0), (0, 128 - heads))), jnp.pad(cum.T, ((0, padded - heads), (0, 0)))


def scan_run(series, cum, input_map, output_map):
    length, channels, heads, width, slab_heads, blocks = scan_sizes(series, cum)
    wide, tall = padded_cum(cum, heads)

    def rows(columns):
        return pl.BlockSpec((SCAN_BLOCK, columns), lambda i: (i, 0))

    return pl.pallas_call(
        functools.partial(scan_forward_kernel, slab_heads, width, heads),
        grid=(blocks,),
        in_specs=[
            rows(channels),
            rows(128),
            pl.BlockSpec((tall.shape[0], SCAN_BLOCK), lambda i: (0, i)),
            rows(STATE),
            rows(STATE),
        ],
        out_specs=[rows(channels), pl.BlockSpec((1, STATE, channels), lambda i: (i, 0, 0))],
        out_shape=[
            jax.ShapeDtypeStruct((length, channels), jnp.float32),
            jax.ShapeDtypeStruct((blocks, STATE, channels), jnp.float32),
        ],
        scratch_shapes=[pltpu.VMEM((STATE, channels), jnp.float32)],
        compiler_params=pltpu.CompilerParams(vmem_limit_bytes=16 * 1024 * 1024),
        cost_estimate=pl.CostEstimate(
            flops=400_000_000, bytes_accessed=4_000_000, transcendentals=800_000
        ),
    )(series, wide, tall, input_map, output_map)


@jax.custom_vjp
def scan_core(series, cum, input_map, output_map):
    return scan_run(series, cum, input_map, output_map)[0]


def scan_core_forward(series, cum, input_map, output_map):
    outputs, saved = scan_run(series, cum, input_map, output_map)
    return outputs, (series, cum, input_map, output_map, saved)


def scan_core_backward(residuals, gradient):
    series, cum, input_map, output_map, saved = residuals
    length, channels, heads, width, slab_heads, blocks = scan_sizes(series, cum)
    wide, tall = padded_cum(cum, heads)

    def rows(columns):
        return pl.BlockSpec((SCAN_BLOCK, columns), lambda i: (blocks - 1 - i, 0))

    across = pl.BlockSpec((tall.shape[0], SCAN_BLOCK), lambda i: (0, blocks - 1 - i))
    d_series, d_wide, d_tall, d_input, d_output = pl.pallas_call(
        functools.partial(scan_backward_kernel, slab_heads, width, heads),
        grid=(blocks,),
        in_specs=[
            rows(channels),
            rows(128),
            across,
            rows(STATE),
            rows(STATE),
            pl.BlockSpec((1, STATE, channels), lambda i: (blocks - 1 - i, 0, 0)),
            rows(channels),
        ],
        out_specs=[rows(channels), rows(128), across, rows(STATE), rows(STATE)],
        out_shape=[
            jax.ShapeDtypeStruct((length, channels), jnp.float32),
            jax.ShapeDtypeStruct((length, 128), jnp.float32),
            jax.ShapeDtypeStruct(tall.shape, jnp.float32),
            jax.ShapeDtypeStruct((length, STATE), jnp.float32),
            jax.ShapeDtypeStruct((length, STATE), jnp.float32),
        ],
        scratch_shapes=[pltpu.VMEM((STATE, channels), jnp.float32)],
        compiler_params=pltpu.CompilerParams(vmem_limit_bytes=16 * 1024 * 1024),
        cost_estimate=pl.CostEstimate(
            flops=2_000_000_000, bytes_accessed=40_000_000, transcendentals=1_600_000
        ),
    )(series, wide, tall, input_map, output_map, saved, gradient)
    return d_series, d_wide[:, :heads] + d_tall[:heads].T, d_input, d_output


scan_core.defvjp(scan_core_forward, scan_core_backward)


def mamba_core(
    gate_proj,
    input_proj,
    state_proj,
    step_proj,
    kernel_local,
    bias_local,
    decay_local,
    step_local,
    skip_local,
):
    length, channel_count = input_proj.shape
    heads_here = step_proj.shape[1]
    activated = jax.nn.silu(
        causal_conv(jnp.concatenate([input_proj, state_proj], 1), kernel_local, bias_local)
    )
    series = activated[:, :channel_count]
    input_map = activated[:, channel_count : channel_count + STATE]
    output_map = activated[:, channel_count + STATE :]
    step_sizes = jax.nn.softplus(step_proj + step_local)
    decay_rates = -jnp.exp(decay_local)
    position = lax.broadcasted_iota(jnp.int32, (SCAN_BLOCK, SCAN_BLOCK), 0)
    earlier = lax.broadcasted_iota(jnp.int32, (SCAN_BLOCK, SCAN_BLOCK), 1)
    cum = jnp.einsum(
        "ts,bsh->bth",
        (position >= earlier).astype(jnp.float32),
        (step_sizes * decay_rates).reshape(-1, SCAN_BLOCK, heads_here),
        precision=highest,
    ).reshape(length, heads_here)
    width = channel_count // heads_here
    scanned = scan_core(
        series * jnp.repeat(step_sizes, width, axis=1), cum, input_map, output_map
    ) + series * jnp.repeat(skip_local, width)
    return scanned * jax.nn.silu(gate_proj)


def partner_pairs(count):
    return [(index, index ^ 1) for index in range(count)]


def shift_pairs(count, steps):
    return [(index, (index + 2 * steps) % count) for index in range(count)]


def gather_dp(piece):
    count = lax.axis_size("dp")
    if count > 8 or count % 2:
        return lax.all_gather(piece, "dp", axis=0, tiled=True)
    mine = lax.axis_index("dp")
    rows = piece.shape[0]
    result = jnp.zeros((count * rows,) + piece.shape[1:], piece.dtype)

    def put(result, block, source):
        return lax.dynamic_update_slice_in_dim(result, block, source * rows, 0)

    far = [lax.ppermute(piece, "dp", shift_pairs(count, steps)) for steps in range(1, count // 2)]
    near = lax.ppermute(piece, "dp", partner_pairs(count))
    crossed = [lax.ppermute(block, "dp", partner_pairs(count)) for block in far]
    other = mine + 1 - 2 * (mine % 2)
    result = put(result, piece, mine)
    result = put(result, near, other)
    for steps in range(1, count // 2):
        result = put(result, far[steps - 1], (mine - 2 * steps + count) % count)
        result = put(result, crossed[steps - 1], (other - 2 * steps + count) % count)
    return result


def reduce_dp(partial):
    count = lax.axis_size("dp")
    rows = partial.shape[0] // count
    if count > 8 or count % 2:
        return lax.psum_scatter(partial, "dp", scatter_dimension=0, tiled=True).astype(jnp.float32)
    mine = lax.axis_index("dp")
    side = mine % 2
    place = mine // 2
    half_count = count // 2
    split = partial.reshape((half_count, 2, rows) + partial.shape[1:])
    sent = lax.dynamic_index_in_dim(split, 1 - side, 1, keepdims=False)
    kept = lax.dynamic_index_in_dim(split, side, 1, keepdims=False)
    arrived = lax.ppermute(sent, "dp", partner_pairs(count))
    paired = (kept.astype(jnp.float32) + arrived.astype(jnp.float32)).astype(jnp.bfloat16)
    total = lax.dynamic_index_in_dim(paired, place, 0, keepdims=False).astype(jnp.float32)
    for steps in range(1, half_count):
        block = lax.dynamic_index_in_dim(paired, (place + steps) % half_count, 0, keepdims=False)
        total = total + lax.ppermute(block, "dp", shift_pairs(count, steps)).astype(jnp.float32)
    return total


def full_rows(local_piece):
    return lax.all_gather(local_piece, "tensor", axis=0, tiled=True)


def summed_rows(operand_pairs, row_count):
    running = jnp.zeros(
        (row_count * lax.axis_size("tensor"), operand_pairs[0][1].shape[0]), jnp.float32
    )
    for left_side, right_side in operand_pairs:
        running = running + lax.dot_general(
            left_side, right_side, by_columns, preferred_element_type=jnp.float32
        )
    return lax.psum_scatter(
        running.astype(jnp.bfloat16), "tensor", scatter_dimension=0, tiled=True
    ).astype(jnp.float32)


def weight_grad(activations, gradient):
    return lax.dot_general(activations, gradient, by_rows, preferred_element_type=jnp.float32)


def block_scores(query_block, key_rot, first_row, score_scale):
    raw_scores = (
        jnp.einsum("qhd,kd->hqk", query_block, key_rot, preferred_element_type=jnp.float32)
        * score_scale
    )
    row_index = first_row + lax.broadcasted_iota(jnp.int32, raw_scores.shape, 1)
    column_index = lax.broadcasted_iota(jnp.int32, raw_scores.shape, 2)
    return jnp.where(column_index <= row_index, raw_scores, -1e30)


def local(
    inputs,
    cotangent,
    mix_gain,
    query_weight,
    key_weight,
    value_weight,
    attention_out,
    mamba_gate,
    mamba_input,
    state_weight,
    step_weight,
    mamba_out,
    kernel_weight,
    kernel_bias,
    decay_log,
    step_bias,
    skip_weight,
    mlp_gain,
    gate_weight,
    up_weight,
    down_weight,
):
    tensor_index = lax.axis_index("tensor")
    local_rows = inputs.shape[0]
    query_heads = query_weight.shape[1] // HEAD_DIM
    key_head = tensor_index * query_heads // (HEADS // KV_HEADS)
    unit_count = gate_weight.shape[1]
    scan_width = mamba_input.shape[1]
    scan_heads = step_weight.shape[1]
    weight_rows = query_weight.shape[0]
    narrow = jnp.concatenate(
        [
            step_weight,
            mix_gain[:, None],
            mlp_gain[:, None],
            jnp.zeros((weight_rows, 128 - scan_heads - 2), jnp.bfloat16),
        ],
        1,
    )
    key_own = lax.dynamic_slice_in_dim(key_weight, key_head * HEAD_DIM, HEAD_DIM, 1)
    value_own = lax.dynamic_slice_in_dim(value_weight, key_head * HEAD_DIM, HEAD_DIM, 1)
    mix_pack = gather_dp(
        jnp.concatenate(
            [mamba_gate, mamba_input, state_weight, query_weight, key_own, value_own, narrow], 1
        )
    )
    out_pack = gather_dp(jnp.concatenate([attention_out, mamba_out], 1))
    mlp_pack = gather_dp(jnp.concatenate([gate_weight, up_weight, down_weight], 1))

    def take(pack, widths):
        pieces, start = [], 0
        for width in widths:
            pieces.append(pack[:, start : start + width])
            start += width
        return pieces

    query_width = query_weight.shape[1]
    gate_ssm_all, input_ssm_all, state_all, query_all, key_slice, value_slice, narrow_all = take(
        mix_pack,
        (scan_width, scan_width, state_weight.shape[1], query_width, HEAD_DIM, HEAD_DIM, 128),
    )
    step_all = narrow_all[:, :scan_heads]
    mix_gain_all = narrow_all[:, scan_heads]
    mlp_gain_all = narrow_all[:, scan_heads + 1]
    attention_all, mamba_out_all = take(out_pack, (query_width, scan_width))
    gate_all, up_all, down_all = take(mlp_pack, (unit_count,) * 3)
    full_width = SSM_HEADS * SSM_HEAD_DIM
    kernel_local = jnp.concatenate(
        [
            lax.dynamic_slice_in_dim(kernel_weight, tensor_index * scan_width, scan_width, 1),
            kernel_weight[:, full_width:],
        ],
        1,
    )
    bias_local = jnp.concatenate(
        [
            lax.dynamic_slice_in_dim(kernel_bias, tensor_index * scan_width, scan_width, 0),
            kernel_bias[full_width:],
        ],
        0,
    )
    decay_local = lax.dynamic_slice_in_dim(decay_log, tensor_index * scan_heads, scan_heads, 0)
    step_local = lax.dynamic_slice_in_dim(step_bias, tensor_index * scan_heads, scan_heads, 0)
    skip_local = lax.dynamic_slice_in_dim(skip_weight, tensor_index * scan_heads, scan_heads, 0)
    rows_float = inputs.astype(jnp.float32)
    normed, first_norm_back = jax.vjp(rms_norm, rows_float, mix_gain_all.astype(jnp.float32))
    normed_local = normed.astype(jnp.bfloat16)
    mixer_rows = full_rows(normed_local)
    length = mixer_rows.shape[0]
    cosine_table, sine_table = rotary_tables(length)
    query_proj = jnp.dot(mixer_rows, query_all, preferred_element_type=jnp.float32).reshape(
        length, query_heads, HEAD_DIM
    )
    key_proj = jnp.dot(mixer_rows, key_slice, preferred_element_type=jnp.float32)
    value_proj = jnp.dot(mixer_rows, value_slice, preferred_element_type=jnp.float32)
    query_rot = rotary(query_proj, cosine_table, sine_table).astype(jnp.bfloat16)
    key_rot = rotary(key_proj[:, None], cosine_table, sine_table)[:, 0].astype(jnp.bfloat16)
    value_low = value_proj.astype(jnp.bfloat16)
    block_rows = min(512, length)
    block_count = length // block_rows
    score_scale = HEAD_DIM ** (-0.5)
    block_ids = jnp.arange(block_count, dtype=jnp.int32)

    def attend_block(block_index):
        first_row = block_index * block_rows
        scores = block_scores(query_rot, key_rot, first_row, score_scale)
        row_max = jnp.max(scores, -1, keepdims=True)
        shifted = jnp.exp(scores - row_max)
        row_total = jnp.sum(shifted, -1, keepdims=True)
        weights_low = (shifted / row_total).astype(jnp.bfloat16)
        attended = jnp.einsum(
            "hqk,kd->qhd", weights_low, value_low, preferred_element_type=jnp.float32
        )
        return (attended, (row_max + jnp.log(row_total))[..., 0])

    attended_blocks, log_totals = lax.map(attend_block, block_ids)
    attended_low = attended_blocks.reshape(length, query_heads * HEAD_DIM).astype(jnp.bfloat16)
    gate_proj = jnp.dot(mixer_rows, gate_ssm_all, preferred_element_type=jnp.float32)
    input_proj = jnp.dot(mixer_rows, input_ssm_all, preferred_element_type=jnp.float32)
    state_proj = jnp.dot(mixer_rows, state_all, preferred_element_type=jnp.float32)
    step_proj = jnp.dot(mixer_rows, step_all, preferred_element_type=jnp.float32)
    gated_out, mamba_back = jax.vjp(
        mamba_core,
        gate_proj,
        input_proj,
        state_proj,
        step_proj,
        kernel_local,
        bias_local,
        decay_local,
        step_local,
        skip_local,
    )
    gated_low = gated_out.astype(jnp.bfloat16)
    mixed = summed_rows(((attended_low, attention_all), (gated_low, mamba_out_all)), local_rows)
    hidden = rows_float + mixed
    normed_mlp, second_norm_back = jax.vjp(rms_norm, hidden, mlp_gain_all.astype(jnp.float32))
    normed_mlp_local = normed_mlp.astype(jnp.bfloat16)
    mlp_rows = full_rows(normed_mlp_local)
    gate_pre = jnp.dot(mlp_rows, gate_all, preferred_element_type=jnp.float32)
    up_pre = jnp.dot(mlp_rows, up_all, preferred_element_type=jnp.float32)
    sigmoid_gate = jax.nn.sigmoid(gate_pre)
    silu_gate = gate_pre * sigmoid_gate
    units_low = (silu_gate * up_pre).astype(jnp.bfloat16)
    mlp_sum = summed_rows(((units_low, down_all),), local_rows)
    output = (hidden + mlp_sum).astype(jnp.bfloat16)
    cotangent_rows = full_rows(cotangent)
    grad_down = weight_grad(cotangent_rows, units_low)
    unit_grad = jnp.dot(cotangent_rows, down_all, preferred_element_type=jnp.float32)
    gate_grad = (
        unit_grad * up_pre * (sigmoid_gate * (1.0 + gate_pre * (1.0 - sigmoid_gate)))
    ).astype(jnp.bfloat16)
    up_grad = (unit_grad * silu_gate).astype(jnp.bfloat16)
    grad_gate = weight_grad(mlp_rows, gate_grad)
    grad_up = weight_grad(mlp_rows, up_grad)
    mlp_input_grad = summed_rows(((gate_grad, gate_all), (up_grad, up_all)), local_rows)
    hidden_norm_grad, grad_mlp_gain = second_norm_back(mlp_input_grad)
    hidden_grad = cotangent.astype(jnp.float32) + hidden_norm_grad
    mixer_grad_rows = full_rows(hidden_grad.astype(jnp.bfloat16))
    grad_attention = weight_grad(mixer_grad_rows, attended_low)
    grad_mamba_out = weight_grad(mixer_grad_rows, gated_low)
    attended_grad = (
        jnp.dot(mixer_grad_rows, attention_all, preferred_element_type=jnp.float32)
        .astype(jnp.bfloat16)
        .reshape(length, query_heads, HEAD_DIM)
    )
    gated_grad = jnp.dot(mixer_grad_rows, mamba_out_all, preferred_element_type=jnp.float32)

    def attend_back(carried, block_index):
        key_total, value_total = carried
        first_row = block_index * block_rows
        scores = block_scores(query_rot, key_rot, first_row, score_scale)
        probabilities = jnp.exp(scores - log_totals[block_index][..., None])
        prob_grad = jnp.einsum(
            "qhd,kd->hqk", attended_grad, value_low, preferred_element_type=jnp.float32
        )
        row_dot = jnp.sum(prob_grad * probabilities, -1, keepdims=True)
        score_grad = (probabilities * (prob_grad - row_dot)).astype(jnp.bfloat16)
        query_grad = (
            jnp.einsum("hqk,kd->qhd", score_grad, key_rot, preferred_element_type=jnp.float32)
            * score_scale
        )
        key_total = (
            key_total
            + jnp.einsum("hqk,qhd->kd", score_grad, query_rot, preferred_element_type=jnp.float32)
            * score_scale
        )
        value_total = value_total + jnp.einsum(
            "hqk,qhd->kd",
            probabilities.astype(jnp.bfloat16),
            attended_grad,
            preferred_element_type=jnp.float32,
        )
        return ((key_total, value_total), query_grad)

    zero_keys = jnp.zeros((length, HEAD_DIM), jnp.float32)
    (key_total, value_total), query_grads = lax.scan(attend_back, (zero_keys, zero_keys), block_ids)
    query_low = (
        unrotate(query_grads.reshape(length, query_heads, HEAD_DIM), cosine_table, sine_table)
        .astype(jnp.bfloat16)
        .reshape(length, query_heads * HEAD_DIM)
    )
    key_low = unrotate(key_total[:, None], cosine_table, sine_table)[:, 0].astype(jnp.bfloat16)
    value_grad_low = value_total.astype(jnp.bfloat16)
    (
        gate_proj_grad,
        input_proj_grad,
        state_proj_grad,
        step_proj_grad,
        kernel_grad,
        bias_grad,
        decay_grad,
        step_bias_grad,
        skip_grad,
    ) = mamba_back(gated_grad)
    gate_proj_low = gate_proj_grad.astype(jnp.bfloat16)
    input_proj_low = input_proj_grad.astype(jnp.bfloat16)
    state_proj_low = state_proj_grad.astype(jnp.bfloat16)
    step_proj_low = step_proj_grad.astype(jnp.bfloat16)
    mixer_input_grad = summed_rows(
        (
            (query_low, query_all),
            (key_low, key_slice),
            (value_grad_low, value_slice),
            (gate_proj_low, gate_ssm_all),
            (input_proj_low, input_ssm_all),
            (state_proj_low, state_all),
            (step_proj_low, step_all),
        ),
        local_rows,
    )
    input_norm_grad, grad_mix_gain = first_norm_back(mixer_input_grad)
    grad_inputs = (hidden_grad + input_norm_grad).astype(jnp.bfloat16)
    grad_query = weight_grad(mixer_rows, query_low)
    key_width = key_weight.shape[1]
    grad_key = lax.dynamic_update_slice_in_dim(
        jnp.zeros((D, key_width), jnp.float32),
        weight_grad(mixer_rows, key_low),
        key_head * HEAD_DIM,
        1,
    )
    grad_value = lax.dynamic_update_slice_in_dim(
        jnp.zeros((D, key_width), jnp.float32),
        weight_grad(mixer_rows, value_grad_low),
        key_head * HEAD_DIM,
        1,
    )
    grad_gate_ssm = weight_grad(mixer_rows, gate_proj_low)
    grad_input_ssm = weight_grad(mixer_rows, input_proj_low)
    grad_state = weight_grad(mixer_rows, state_proj_low)
    grad_step = weight_grad(mixer_rows, step_proj_low)
    count = lax.axis_size("dp")
    tensor_size = lax.axis_size("tensor")
    low = jnp.bfloat16
    shared = jnp.concatenate(
        [
            grad_key,
            grad_value,
            grad_state,
            grad_mix_gain[:, None],
            grad_mlp_gain[:, None],
            jnp.zeros((D, 126), jnp.float32),
        ],
        1,
    ).astype(low)
    shared_width = shared.shape[1]
    shared = lax.psum_scatter(
        shared.reshape(count, tensor_size, D // count // tensor_size, shared_width),
        "tensor",
        scatter_dimension=1,
        tiled=True,
    )
    shared = shared.reshape(D, shared_width // tensor_size)
    mlp_sum_pack = reduce_dp(jnp.concatenate([grad_gate, grad_up, grad_down], 1).astype(low))
    out_sum_pack = reduce_dp(jnp.concatenate([grad_attention, grad_mamba_out], 1).astype(low))
    mix_sum_pack = reduce_dp(
        jnp.concatenate(
            [
                grad_gate_ssm.astype(low),
                grad_input_ssm.astype(low),
                grad_query.astype(low),
                shared,
                grad_step.astype(low),
            ],
            1,
        )
    )
    mlp_sums = take(mlp_sum_pack, (unit_count,) * 3)
    attention_sum, mamba_out_sum = take(out_sum_pack, (query_width, scan_width))
    gate_ssm_sum, input_ssm_sum, query_sum, shared_sum, step_sum = take(
        mix_sum_pack,
        (scan_width, scan_width, query_width, shared_width // tensor_size, scan_heads),
    )
    shared_sum = shared_sum.reshape(D // count // tensor_size, shared_width)
    key_sum, value_sum, state_sum = take(
        shared_sum, (key_width, key_width, state_weight.shape[1])
    )
    mix_gain_sum = shared_sum[:, shared_width - 128]
    mlp_gain_sum = shared_sum[:, shared_width - 127]
    mix_sums = (query_sum, attention_sum, gate_ssm_sum, input_ssm_sum, step_sum, mamba_out_sum)
    shared_sums = (mix_gain_sum, mlp_gain_sum, key_sum, value_sum, state_sum)
    small_own = jnp.concatenate(
        [kernel_grad.reshape(-1), bias_grad, decay_grad, step_bias_grad, skip_grad]
    )
    small_rows = -(-small_own.shape[0] // 1024) * 8
    small_own = jnp.pad(small_own, (0, small_rows * 128 - small_own.shape[0]))
    small_every = lax.all_gather(
        small_own.reshape(small_rows, 128), ("dp", "tensor"), axis=0, tiled=True
    )
    small_tensor = jnp.sum(small_every.reshape(count, tensor_size, -1), 0)
    local_width = kernel_grad.shape[1]
    taps = small_tensor[:, : KCONV * local_width].reshape(tensor_size, KCONV, local_width)
    bias_start = KCONV * local_width
    biases = small_tensor[:, bias_start : bias_start + local_width]
    small_sums = [
        jnp.concatenate(
            [
                taps[:, :, :scan_width].transpose(1, 0, 2).reshape(KCONV, full_width),
                jnp.sum(taps[:, :, scan_width:], 0),
            ],
            1,
        ),
        jnp.concatenate([biases[:, :scan_width].reshape(-1), jnp.sum(biases[:, scan_width:], 0)]),
    ]
    start = bias_start + local_width
    for _ in range(3):
        small_sums.append(small_tensor[:, start : start + scan_heads].reshape(-1))
        start += scan_heads
    return (
        output,
        grad_inputs,
        shared_sums[0],
        mix_sums[0],
        shared_sums[2],
        shared_sums[3],
        mix_sums[1],
        mix_sums[2],
        mix_sums[3],
        shared_sums[4],
        mix_sums[4],
        mix_sums[5],
        small_sums[0],
        small_sums[1],
        small_sums[2],
        small_sums[3],
        small_sums[4],
        shared_sums[1],
        mlp_sums[0],
        mlp_sums[1],
        mlp_sums[2],
    )


def solution(mesh):
    placed = (
        P(("dp", "tensor"), None),
        P(("dp", "tensor"), None),
        P("dp"),
        P("dp", "tensor"),
        P("dp", None),
        P("dp", None),
        P("dp", "tensor"),
        P("dp", "tensor"),
        P("dp", "tensor"),
        P("dp", None),
        P("dp", "tensor"),
        P("dp", "tensor"),
        P(),
        P(),
        P(),
        P(),
        P(),
        P("dp"),
        P("dp", "tensor"),
        P("dp", "tensor"),
        P("dp", "tensor"),
    )
    return jax.shard_map(
        local,
        mesh=mesh,
        in_specs=placed,
        out_specs=(
            P(("dp", "tensor"), None),
            P(("dp", "tensor"), None),
            P(("dp", "tensor")),
            P("dp", "tensor"),
            P(("dp", "tensor"), None),
            P(("dp", "tensor"), None),
            P("dp", "tensor"),
            P("dp", "tensor"),
            P("dp", "tensor"),
            P(("dp", "tensor"), None),
            P("dp", "tensor"),
            P("dp", "tensor"),
            P(),
            P(),
            P(),
            P(),
            P(),
            P(("dp", "tensor")),
            P("dp", "tensor"),
            P("dp", "tensor"),
            P("dp", "tensor"),
        ),
        check_vma=False,
    )
```

```python
import functools
import math

import jax
import jax.numpy as jnp
from jax import lax
from jax.experimental import pallas as pl
from jax.experimental.pallas import tpu as pltpu
from jax.sharding import PartitionSpec as P

D = 1024
HEADS = 8
KV_HEADS = 2
HEAD_DIM = 64
SSM_HEADS = 24
SSM_HEAD_DIM = 64
STATE = 128
KCONV = 4
SCAN_BLOCK = 128


eps = 1e-05
rope_base = 100000000000.0
highest = lax.Precision.HIGHEST
by_rows = (((0,), (0,)), ((), ()))
by_columns = (((1,), (1,)), ((), ()))


def rms_norm(values, gain_vector):
    return values * lax.rsqrt(jnp.mean(values * values, -1, keepdims=True) + eps) * gain_vector


def rotary_tables(length):
    half_dim = HEAD_DIM // 2
    frequency = jnp.exp(
        jnp.arange(half_dim, dtype=jnp.float32) * (-2.0 * math.log(rope_base) / HEAD_DIM)
    )
    angles = jnp.arange(length, dtype=jnp.float32)[:, None] * frequency[None, :]
    return (jnp.cos(angles)[:, None, :], jnp.sin(angles)[:, None, :])


def rotary(values, cosine_table, sine_table):
    half_dim = values.shape[-1] // 2
    former = values[..., :half_dim]
    latter = values[..., half_dim:]
    return jnp.concatenate(
        [former * cosine_table - latter * sine_table, latter * cosine_table + former * sine_table],
        -1,
    )


def unrotate(gradient, cosine_table, sine_table):
    half_dim = gradient.shape[-1] // 2
    former = gradient[..., :half_dim]
    latter = gradient[..., half_dim:]
    return jnp.concatenate(
        [former * cosine_table + latter * sine_table, latter * cosine_table - former * sine_table],
        -1,
    )


def causal_conv(signal, kernel, offset):
    length = signal.shape[0]
    tap_count = kernel.shape[0]
    padded = jnp.concatenate(
        [jnp.zeros((tap_count - 1,) + signal.shape[1:], signal.dtype), signal], 0
    )
    result = offset
    for lag_index in range(tap_count):
        result = result + kernel[lag_index] * padded[lag_index : lag_index + length]
    return result


def low_dot(left, right, dims):
    return lax.dot_general(
        left.astype(jnp.bfloat16),
        right.astype(jnp.bfloat16),
        dims,
        preferred_element_type=jnp.float32,
    )


plain = (((1,), (0,)), ((), ()))


def head_lanes(values, first_head, heads, width):
    rows = values.shape[0]
    lane = lax.broadcasted_iota(jnp.int32, (rows, heads * width), 1)
    spread = jnp.broadcast_to(values[:, first_head : first_head + 1], lane.shape)
    for index in range(1, heads):
        column = first_head + index
        spread = jnp.where(
            lane < index * width,
            spread,
            jnp.broadcast_to(values[:, column : column + 1], lane.shape),
        )
    return spread


def decay_weights(column, row):
    size = column.shape[0]
    later = lax.broadcasted_iota(jnp.int32, (size, size), 0)
    earlier = lax.broadcasted_iota(jnp.int32, (size, size), 1)
    return jnp.exp(jnp.where(later >= earlier, column - row, -1e30))


def scan_forward_kernel(
    slab_heads, width, heads, x_ref, cum_ref, cumt_ref, b_ref, c_ref, y_ref, saved_ref, state_ref
):
    @pl.when(pl.program_id(0) == 0)
    def _():
        state_ref[...] = jnp.zeros_like(state_ref)

    size = x_ref.shape[0]
    slab = slab_heads * width
    saved_ref[0] = state_ref[...]
    cum = cum_ref[...]
    input_map, output_map = b_ref[...], c_ref[...]
    affinity = low_dot(output_map, input_map, by_columns)
    lane = lax.broadcasted_iota(jnp.int32, (size, slab), 1)
    for first in range(0, heads, slab_heads):
        cols = slice(first * width, first * width + slab)
        series = x_ref[:, cols]
        state = state_ref[:, cols]
        spread = head_lanes(cum, first, slab_heads, width)
        last = spread[size - 1 : size]
        result = low_dot(output_map, state, plain) * jnp.exp(spread)
        for index in range(slab_heads):
            head = first + index
            decay = decay_weights(cum[:, head : head + 1], cumt_ref[head : head + 1, :])
            own = (lane >= index * width) & (lane < (index + 1) * width)
            result = result + low_dot(decay * affinity, jnp.where(own, series, 0.0), plain)
        y_ref[:, cols] = result
        state_ref[:, cols] = state * jnp.exp(last) + low_dot(
            input_map, series * jnp.exp(last - spread), by_rows
        )


def scan_backward_kernel(
    slab_heads,
    width,
    heads,
    x_ref,
    cum_ref,
    cumt_ref,
    b_ref,
    c_ref,
    saved_ref,
    g_ref,
    dx_ref,
    dcum_ref,
    dcumt_ref,
    db_ref,
    dc_ref,
    state_ref,
):
    @pl.when(pl.program_id(0) == 0)
    def _():
        state_ref[...] = jnp.zeros_like(state_ref)

    size = x_ref.shape[0]
    slab = slab_heads * width
    cum = cum_ref[...]
    input_map, output_map = b_ref[...], c_ref[...]
    affinity = low_dot(output_map, input_map, by_columns)
    lane = lax.broadcasted_iota(jnp.int32, (size, slab), 1)
    cum_lane = lax.broadcasted_iota(jnp.int32, cum.shape, 1)
    cum_row = lax.broadcasted_iota(jnp.int32, cum.shape, 0)
    d_cum = jnp.zeros(cum.shape, jnp.float32)
    d_affinity = jnp.zeros((size, size), jnp.float32)
    d_input = jnp.zeros(input_map.shape, jnp.float32)
    d_output = jnp.zeros(output_map.shape, jnp.float32)
    dcumt_ref[...] = jnp.zeros_like(dcumt_ref)
    for first in range(0, heads, slab_heads):
        cols = slice(first * width, first * width + slab)
        series = x_ref[:, cols]
        gradient = g_ref[:, cols]
        state = saved_ref[0, :, cols]
        d_state = state_ref[:, cols]
        spread = head_lanes(cum, first, slab_heads, width)
        last = spread[size - 1 : size]
        remain = jnp.exp(last - spread)
        grown = gradient * jnp.exp(spread)
        kept = series * remain
        d_kept = low_dot(input_map, d_state, plain)
        d_output = d_output + low_dot(grown, state, by_columns)
        d_input = d_input + low_dot(kept, d_state, by_columns)
        written = d_kept * kept
        position = grown * low_dot(output_map, state, plain) - written
        decayed = d_state * jnp.exp(last)
        final = jnp.sum(decayed * state, 0, keepdims=True) + jnp.sum(written, 0, keepdims=True)
        d_series = d_kept * remain
        for index in range(slab_heads):
            head = first + index
            decay = decay_weights(cum[:, head : head + 1], cumt_ref[head : head + 1, :])
            own = (lane >= index * width) & (lane < (index + 1) * width)
            own_gradient = jnp.where(own, gradient, 0.0)
            d_weights = low_dot(own_gradient, series, by_columns) * decay
            d_affinity = d_affinity + d_weights
            d_gaps = d_weights * affinity
            d_series = d_series + low_dot(decay * affinity, own_gradient, by_rows)
            column = jnp.sum(d_gaps, 1, keepdims=True) + jnp.sum(
                jnp.where(own, position, 0.0), 1, keepdims=True
            )
            total = jnp.sum(jnp.where(own[:1], final, 0.0), 1, keepdims=True)
            column = jnp.where(cum_row == size - 1, column + total, column)
            d_cum = jnp.where(cum_lane == head, column, d_cum)
            dcumt_ref[head : head + 1, :] = -jnp.sum(d_gaps, 0, keepdims=True)
        dx_ref[:, cols] = d_series
        state_ref[:, cols] = decayed + low_dot(output_map, grown, by_rows)
    dcum_ref[...] = d_cum
    db_ref[...] = d_input + low_dot(d_affinity, output_map, by_rows)
    dc_ref[...] = d_output + low_dot(d_affinity, input_map, plain)


def scan_sizes(series, cum):
    length, channels = series.shape
    heads = cum.shape[1]
    width = channels // heads
    slab_heads = max(1, 128 // width)
    while heads % slab_heads:
        slab_heads -= 1
    return length, channels, heads, width, slab_heads, length // SCAN_BLOCK


def padded_cum(cum, heads):
    padded = -(-heads // 8) * 8
    return jnp.pad(cum, ((0, 0), (0, 128 - heads))), jnp.pad(cum.T, ((0, padded - heads), (0, 0)))


def scan_run(series, cum, input_map, output_map):
    length, channels, heads, width, slab_heads, blocks = scan_sizes(series, cum)
    wide, tall = padded_cum(cum, heads)

    def rows(columns):
        return pl.BlockSpec((SCAN_BLOCK, columns), lambda i: (i, 0))

    return pl.pallas_call(
        functools.partial(scan_forward_kernel, slab_heads, width, heads),
        grid=(blocks,),
        in_specs=[
            rows(channels),
            rows(128),
            pl.BlockSpec((tall.shape[0], SCAN_BLOCK), lambda i: (0, i)),
            rows(STATE),
            rows(STATE),
        ],
        out_specs=[rows(channels), pl.BlockSpec((1, STATE, channels), lambda i: (i, 0, 0))],
        out_shape=[
            jax.ShapeDtypeStruct((length, channels), jnp.float32),
            jax.ShapeDtypeStruct((blocks, STATE, channels), jnp.float32),
        ],
        scratch_shapes=[pltpu.VMEM((STATE, channels), jnp.float32)],
        compiler_params=pltpu.CompilerParams(vmem_limit_bytes=16 * 1024 * 1024),
        cost_estimate=pl.CostEstimate(
            flops=400_000_000, bytes_accessed=4_000_000, transcendentals=800_000
        ),
    )(series, wide, tall, input_map, output_map)


@jax.custom_vjp
def scan_core(series, cum, input_map, output_map):
    return scan_run(series, cum, input_map, output_map)[0]


def scan_core_forward(series, cum, input_map, output_map):
    outputs, saved = scan_run(series, cum, input_map, output_map)
    return outputs, (series, cum, input_map, output_map, saved)


def scan_core_backward(residuals, gradient):
    series, cum, input_map, output_map, saved = residuals
    length, channels, heads, width, slab_heads, blocks = scan_sizes(series, cum)
    wide, tall = padded_cum(cum, heads)

    def rows(columns):
        return pl.BlockSpec((SCAN_BLOCK, columns), lambda i: (blocks - 1 - i, 0))

    across = pl.BlockSpec((tall.shape[0], SCAN_BLOCK), lambda i: (0, blocks - 1 - i))
    d_series, d_wide, d_tall, d_input, d_output = pl.pallas_call(
        functools.partial(scan_backward_kernel, slab_heads, width, heads),
        grid=(blocks,),
        in_specs=[
            rows(channels),
            rows(128),
            across,
            rows(STATE),
            rows(STATE),
            pl.BlockSpec((1, STATE, channels), lambda i: (blocks - 1 - i, 0, 0)),
            rows(channels),
        ],
        out_specs=[rows(channels), rows(128), across, rows(STATE), rows(STATE)],
        out_shape=[
            jax.ShapeDtypeStruct((length, channels), jnp.float32),
            jax.ShapeDtypeStruct((length, 128), jnp.float32),
            jax.ShapeDtypeStruct(tall.shape, jnp.float32),
            jax.ShapeDtypeStruct((length, STATE), jnp.float32),
            jax.ShapeDtypeStruct((length, STATE), jnp.float32),
        ],
        scratch_shapes=[pltpu.VMEM((STATE, channels), jnp.float32)],
        compiler_params=pltpu.CompilerParams(vmem_limit_bytes=16 * 1024 * 1024),
        cost_estimate=pl.CostEstimate(
            flops=2_000_000_000, bytes_accessed=40_000_000, transcendentals=1_600_000
        ),
    )(series, wide, tall, input_map, output_map, saved, gradient)
    return d_series, d_wide[:, :heads] + d_tall[:heads].T, d_input, d_output


scan_core.defvjp(scan_core_forward, scan_core_backward)


def mamba_core(
    gate_proj,
    input_proj,
    state_proj,
    step_proj,
    kernel_local,
    bias_local,
    decay_local,
    step_local,
    skip_local,
):
    length, channel_count = input_proj.shape
    heads_here = step_proj.shape[1]
    activated = jax.nn.silu(
        causal_conv(jnp.concatenate([input_proj, state_proj], 1), kernel_local, bias_local)
    )
    series = activated[:, :channel_count]
    input_map = activated[:, channel_count : channel_count + STATE]
    output_map = activated[:, channel_count + STATE :]
    step_sizes = jax.nn.softplus(step_proj + step_local)
    decay_rates = -jnp.exp(decay_local)
    position = lax.broadcasted_iota(jnp.int32, (SCAN_BLOCK, SCAN_BLOCK), 0)
    earlier = lax.broadcasted_iota(jnp.int32, (SCAN_BLOCK, SCAN_BLOCK), 1)
    cum = jnp.einsum(
        "ts,bsh->bth",
        (position >= earlier).astype(jnp.float32),
        (step_sizes * decay_rates).reshape(-1, SCAN_BLOCK, heads_here),
        precision=highest,
    ).reshape(length, heads_here)
    width = channel_count // heads_here
    scanned = scan_core(
        series * jnp.repeat(step_sizes, width, axis=1), cum, input_map, output_map
    ) + series * jnp.repeat(skip_local, width)
    return scanned * jax.nn.silu(gate_proj)


def partner_pairs(count):
    return [(index, index ^ 1) for index in range(count)]


def shift_pairs(count, steps):
    return [(index, (index + 2 * steps) % count) for index in range(count)]


def gather_far(piece):
    count = lax.axis_size("dp")
    if not staged(count):
        return [piece]
    far = [lax.ppermute(piece, "dp", shift_pairs(count, steps)) for steps in range(1, count // 2)]
    near = lax.ppermute(piece, "dp", partner_pairs(count))
    return [piece, near] + far


def gather_dp(piece):
    return gather_rest(gather_far(piece))


def gather_rest(parts):
    piece = parts[0]
    count = lax.axis_size("dp")
    if not staged(count):
        return lax.all_gather(piece, "dp", axis=0, tiled=True)
    near, far = parts[1], parts[2:]
    mine = lax.axis_index("dp")
    rows = piece.shape[0]
    result = jnp.zeros((count * rows,) + piece.shape[1:], piece.dtype)

    def put(result, block, source):
        return lax.dynamic_update_slice_in_dim(result, block, source * rows, 0)

    crossed = [lax.ppermute(block, "dp", partner_pairs(count)) for block in far]
    other = mine + 1 - 2 * (mine % 2)
    result = put(result, piece, mine)
    result = put(result, near, other)
    for steps in range(1, count // 2):
        result = put(result, far[steps - 1], (mine - 2 * steps + count) % count)
        result = put(result, crossed[steps - 1], (other - 2 * steps + count) % count)
    return result


def staged(count):
    return count <= 8 and count % 2 == 0


def reduce_pair(partial):
    count = lax.axis_size("dp")
    if not staged(count):
        return partial
    rows = partial.shape[0] // count
    side = lax.axis_index("dp") % 2
    split = partial.reshape((count // 2, 2, rows) + partial.shape[1:])
    sent = lax.dynamic_index_in_dim(split, 1 - side, 1, keepdims=False)
    kept = lax.dynamic_index_in_dim(split, side, 1, keepdims=False)
    arrived = lax.ppermute(sent, "dp", partner_pairs(count))
    return (kept.astype(jnp.float32) + arrived.astype(jnp.float32)).astype(jnp.bfloat16)


def reduce_far(paired):
    count = lax.axis_size("dp")
    if not staged(count):
        return lax.psum_scatter(paired, "dp", scatter_dimension=0, tiled=True).astype(jnp.float32)
    place = lax.axis_index("dp") // 2
    half_count = count // 2
    total = lax.dynamic_index_in_dim(paired, place, 0, keepdims=False).astype(jnp.float32)
    for steps in range(1, half_count):
        block = lax.dynamic_index_in_dim(paired, (place + steps) % half_count, 0, keepdims=False)
        total = total + lax.ppermute(block, "dp", shift_pairs(count, steps)).astype(jnp.float32)
    return total


def full_rows(local_piece):
    return lax.all_gather(local_piece, "tensor", axis=0, tiled=True)


def summed_rows(operand_pairs, row_count):
    running = jnp.zeros(
        (row_count * lax.axis_size("tensor"), operand_pairs[0][1].shape[0]), jnp.float32
    )
    for left_side, right_side in operand_pairs:
        running = running + lax.dot_general(
            left_side, right_side, by_columns, preferred_element_type=jnp.float32
        )
    return lax.psum_scatter(
        running.astype(jnp.bfloat16), "tensor", scatter_dimension=0, tiled=True
    ).astype(jnp.float32)


def weight_grad(activations, gradient):
    return lax.dot_general(activations, gradient, by_rows, preferred_element_type=jnp.float32)


def block_scores(query_block, key_rot, first_row, score_scale):
    raw_scores = (
        jnp.einsum("qhd,kd->hqk", query_block, key_rot, preferred_element_type=jnp.float32)
        * score_scale
    )
    row_index = first_row + lax.broadcasted_iota(jnp.int32, raw_scores.shape, 1)
    column_index = lax.broadcasted_iota(jnp.int32, raw_scores.shape, 2)
    return jnp.where(column_index <= row_index, raw_scores, -1e30)


def local(
    inputs,
    cotangent,
    mix_gain,
    query_weight,
    key_weight,
    value_weight,
    attention_out,
    mamba_gate,
    mamba_input,
    state_weight,
    step_weight,
    mamba_out,
    kernel_weight,
    kernel_bias,
    decay_log,
    step_bias,
    skip_weight,
    mlp_gain,
    gate_weight,
    up_weight,
    down_weight,
):
    tensor_index = lax.axis_index("tensor")
    local_rows = inputs.shape[0]
    query_heads = query_weight.shape[1] // HEAD_DIM
    key_head = tensor_index * query_heads // (HEADS // KV_HEADS)
    unit_count = gate_weight.shape[1]
    scan_width = mamba_input.shape[1]
    scan_heads = step_weight.shape[1]
    weight_rows = query_weight.shape[0]
    narrow = jnp.concatenate(
        [
            step_weight,
            mix_gain[:, None],
            mlp_gain[:, None],
            jnp.zeros((weight_rows, 128 - scan_heads - 2), jnp.bfloat16),
        ],
        1,
    )
    key_own = lax.dynamic_slice_in_dim(key_weight, key_head * HEAD_DIM, HEAD_DIM, 1)
    value_own = lax.dynamic_slice_in_dim(value_weight, key_head * HEAD_DIM, HEAD_DIM, 1)
    mix_pack = gather_dp(
        jnp.concatenate(
            [mamba_gate, mamba_input, state_weight, query_weight, key_own, value_own, narrow], 1
        )
    )
    mix_pack, out_own, mlp_own = lax.optimization_barrier(
        (
            mix_pack,
            jnp.concatenate([attention_out, mamba_out], 1),
            jnp.concatenate([gate_weight, up_weight, down_weight], 1),
        )
    )
    out_pack = gather_dp(out_own)
    mlp_parts = gather_far(mlp_own)

    def take(pack, widths):
        pieces, start = [], 0
        for width in widths:
            pieces.append(pack[:, start : start + width])
            start += width
        return pieces

    query_width = query_weight.shape[1]
    gate_ssm_all, input_ssm_all, state_all, query_all, key_slice, value_slice, narrow_all = take(
        mix_pack,
        (scan_width, scan_width, state_weight.shape[1], query_width, HEAD_DIM, HEAD_DIM, 128),
    )
    step_all = narrow_all[:, :scan_heads]
    mix_gain_all = narrow_all[:, scan_heads]
    mlp_gain_all = narrow_all[:, scan_heads + 1]
    attention_all, mamba_out_all = take(out_pack, (query_width, scan_width))
    full_width = SSM_HEADS * SSM_HEAD_DIM
    kernel_local = jnp.concatenate(
        [
            lax.dynamic_slice_in_dim(kernel_weight, tensor_index * scan_width, scan_width, 1),
            kernel_weight[:, full_width:],
        ],
        1,
    )
    bias_local = jnp.concatenate(
        [
            lax.dynamic_slice_in_dim(kernel_bias, tensor_index * scan_width, scan_width, 0),
            kernel_bias[full_width:],
        ],
        0,
    )
    decay_local = lax.dynamic_slice_in_dim(decay_log, tensor_index * scan_heads, scan_heads, 0)
    step_local = lax.dynamic_slice_in_dim(step_bias, tensor_index * scan_heads, scan_heads, 0)
    skip_local = lax.dynamic_slice_in_dim(skip_weight, tensor_index * scan_heads, scan_heads, 0)
    rows_float = inputs.astype(jnp.float32)
    normed, first_norm_back = jax.vjp(rms_norm, rows_float, mix_gain_all.astype(jnp.float32))
    normed_local = normed.astype(jnp.bfloat16)
    mixer_rows = full_rows(normed_local)
    length = mixer_rows.shape[0]
    cosine_table, sine_table = rotary_tables(length)
    query_proj = jnp.dot(mixer_rows, query_all, preferred_element_type=jnp.float32).reshape(
        length, query_heads, HEAD_DIM
    )
    key_proj = jnp.dot(mixer_rows, key_slice, preferred_element_type=jnp.float32)
    value_proj = jnp.dot(mixer_rows, value_slice, preferred_element_type=jnp.float32)
    query_rot = rotary(query_proj, cosine_table, sine_table).astype(jnp.bfloat16)
    key_rot = rotary(key_proj[:, None], cosine_table, sine_table)[:, 0].astype(jnp.bfloat16)
    value_low = value_proj.astype(jnp.bfloat16)
    block_rows = min(512, length)
    block_count = length // block_rows
    score_scale = HEAD_DIM ** (-0.5)
    block_ids = jnp.arange(block_count, dtype=jnp.int32)

    def attend_block(block_index):
        first_row = block_index * block_rows
        scores = block_scores(query_rot, key_rot, first_row, score_scale)
        row_max = jnp.max(scores, -1, keepdims=True)
        shifted = jnp.exp(scores - row_max)
        row_total = jnp.sum(shifted, -1, keepdims=True)
        weights_low = (shifted / row_total).astype(jnp.bfloat16)
        attended = jnp.einsum(
            "hqk,kd->qhd", weights_low, value_low, preferred_element_type=jnp.float32
        )
        return (attended, (row_max + jnp.log(row_total))[..., 0])

    attended_blocks, log_totals = lax.map(attend_block, block_ids)
    attended_low = attended_blocks.reshape(length, query_heads * HEAD_DIM).astype(jnp.bfloat16)
    gate_proj = jnp.dot(mixer_rows, gate_ssm_all, preferred_element_type=jnp.float32)
    input_proj = jnp.dot(mixer_rows, input_ssm_all, preferred_element_type=jnp.float32)
    state_proj = jnp.dot(mixer_rows, state_all, preferred_element_type=jnp.float32)
    step_proj = jnp.dot(mixer_rows, step_all, preferred_element_type=jnp.float32)
    gated_out, mamba_back = jax.vjp(
        mamba_core,
        gate_proj,
        input_proj,
        state_proj,
        step_proj,
        kernel_local,
        bias_local,
        decay_local,
        step_local,
        skip_local,
    )
    gated_low, mlp_parts = lax.optimization_barrier(
        (gated_out.astype(jnp.bfloat16), mlp_parts)
    )
    gate_all, up_all, down_all = take(gather_rest(mlp_parts), (unit_count,) * 3)
    mixed = summed_rows(((attended_low, attention_all), (gated_low, mamba_out_all)), local_rows)
    hidden = rows_float + mixed
    normed_mlp, second_norm_back = jax.vjp(rms_norm, hidden, mlp_gain_all.astype(jnp.float32))
    normed_mlp_local = normed_mlp.astype(jnp.bfloat16)
    mlp_rows = full_rows(normed_mlp_local)
    gate_pre = jnp.dot(mlp_rows, gate_all, preferred_element_type=jnp.float32)
    up_pre = jnp.dot(mlp_rows, up_all, preferred_element_type=jnp.float32)
    sigmoid_gate = jax.nn.sigmoid(gate_pre)
    silu_gate = gate_pre * sigmoid_gate
    units_low = (silu_gate * up_pre).astype(jnp.bfloat16)
    mlp_sum = summed_rows(((units_low, down_all),), local_rows)
    output = (hidden + mlp_sum).astype(jnp.bfloat16)
    cotangent_rows = full_rows(cotangent)
    grad_down = weight_grad(cotangent_rows, units_low)
    unit_grad = jnp.dot(cotangent_rows, down_all, preferred_element_type=jnp.float32)
    gate_grad = (
        unit_grad * up_pre * (sigmoid_gate * (1.0 + gate_pre * (1.0 - sigmoid_gate)))
    ).astype(jnp.bfloat16)
    up_grad = (unit_grad * silu_gate).astype(jnp.bfloat16)
    grad_gate = weight_grad(mlp_rows, gate_grad)
    grad_up = weight_grad(mlp_rows, up_grad)
    low = jnp.bfloat16
    mlp_paired = reduce_pair(jnp.concatenate([grad_gate, grad_up, grad_down], 1).astype(low))
    mlp_input_grad = summed_rows(((gate_grad, gate_all), (up_grad, up_all)), local_rows)
    hidden_norm_grad, grad_mlp_gain = second_norm_back(mlp_input_grad)
    hidden_grad = cotangent.astype(jnp.float32) + hidden_norm_grad
    mixer_grad_rows = full_rows(hidden_grad.astype(jnp.bfloat16))
    grad_attention = weight_grad(mixer_grad_rows, attended_low)
    grad_mamba_out = weight_grad(mixer_grad_rows, gated_low)
    out_paired = reduce_pair(jnp.concatenate([grad_attention, grad_mamba_out], 1).astype(low))
    attended_grad = (
        jnp.dot(mixer_grad_rows, attention_all, preferred_element_type=jnp.float32)
        .astype(jnp.bfloat16)
        .reshape(length, query_heads, HEAD_DIM)
    )
    gated_grad = jnp.dot(mixer_grad_rows, mamba_out_all, preferred_element_type=jnp.float32)

    def attend_back(carried, block_index):
        key_total, value_total = carried
        first_row = block_index * block_rows
        scores = block_scores(query_rot, key_rot, first_row, score_scale)
        probabilities = jnp.exp(scores - log_totals[block_index][..., None])
        prob_grad = jnp.einsum(
            "qhd,kd->hqk", attended_grad, value_low, preferred_element_type=jnp.float32
        )
        row_dot = jnp.sum(prob_grad * probabilities, -1, keepdims=True)
        score_grad = (probabilities * (prob_grad - row_dot)).astype(jnp.bfloat16)
        query_grad = (
            jnp.einsum("hqk,kd->qhd", score_grad, key_rot, preferred_element_type=jnp.float32)
            * score_scale
        )
        key_total = (
            key_total
            + jnp.einsum("hqk,qhd->kd", score_grad, query_rot, preferred_element_type=jnp.float32)
            * score_scale
        )
        value_total = value_total + jnp.einsum(
            "hqk,qhd->kd",
            probabilities.astype(jnp.bfloat16),
            attended_grad,
            preferred_element_type=jnp.float32,
        )
        return ((key_total, value_total), query_grad)

    zero_keys = jnp.zeros((length, HEAD_DIM), jnp.float32)
    (key_total, value_total), query_grads = lax.scan(attend_back, (zero_keys, zero_keys), block_ids)
    query_low = (
        unrotate(query_grads.reshape(length, query_heads, HEAD_DIM), cosine_table, sine_table)
        .astype(jnp.bfloat16)
        .reshape(length, query_heads * HEAD_DIM)
    )
    key_low = unrotate(key_total[:, None], cosine_table, sine_table)[:, 0].astype(jnp.bfloat16)
    value_grad_low = value_total.astype(jnp.bfloat16)
    (
        gate_proj_grad,
        input_proj_grad,
        state_proj_grad,
        step_proj_grad,
        kernel_grad,
        bias_grad,
        decay_grad,
        step_bias_grad,
        skip_grad,
    ) = mamba_back(gated_grad)
    gate_proj_low = gate_proj_grad.astype(jnp.bfloat16)
    input_proj_low = input_proj_grad.astype(jnp.bfloat16)
    state_proj_low = state_proj_grad.astype(jnp.bfloat16)
    step_proj_low = step_proj_grad.astype(jnp.bfloat16)
    gate_proj_low, input_proj_low, mlp_paired, out_paired = lax.optimization_barrier(
        (gate_proj_low, input_proj_low, mlp_paired, out_paired)
    )
    mlp_sum_pack = reduce_far(mlp_paired)
    out_sum_pack = reduce_far(out_paired)
    mixer_input_grad = summed_rows(
        (
            (query_low, query_all),
            (key_low, key_slice),
            (value_grad_low, value_slice),
            (gate_proj_low, gate_ssm_all),
            (input_proj_low, input_ssm_all),
            (state_proj_low, state_all),
            (step_proj_low, step_all),
        ),
        local_rows,
    )
    input_norm_grad, grad_mix_gain = first_norm_back(mixer_input_grad)
    grad_inputs = (hidden_grad + input_norm_grad).astype(jnp.bfloat16)
    grad_query = weight_grad(mixer_rows, query_low)
    key_width = key_weight.shape[1]
    grad_key = lax.dynamic_update_slice_in_dim(
        jnp.zeros((D, key_width), jnp.float32),
        weight_grad(mixer_rows, key_low),
        key_head * HEAD_DIM,
        1,
    )
    grad_value = lax.dynamic_update_slice_in_dim(
        jnp.zeros((D, key_width), jnp.float32),
        weight_grad(mixer_rows, value_grad_low),
        key_head * HEAD_DIM,
        1,
    )
    grad_gate_ssm = weight_grad(mixer_rows, gate_proj_low)
    grad_input_ssm = weight_grad(mixer_rows, input_proj_low)
    grad_state = weight_grad(mixer_rows, state_proj_low)
    grad_step = weight_grad(mixer_rows, step_proj_low)
    count = lax.axis_size("dp")
    tensor_size = lax.axis_size("tensor")
    shared = jnp.concatenate(
        [
            grad_key,
            grad_value,
            grad_state,
            grad_mix_gain[:, None],
            grad_mlp_gain[:, None],
            jnp.zeros((D, 126), jnp.float32),
        ],
        1,
    ).astype(low)
    shared_width = shared.shape[1]
    shared = lax.psum_scatter(
        shared.reshape(count, tensor_size, D // count // tensor_size, shared_width),
        "tensor",
        scatter_dimension=1,
        tiled=True,
    )
    shared = shared.reshape(D, shared_width // tensor_size)
    mix_paired = reduce_pair(
        jnp.concatenate(
            [
                grad_gate_ssm.astype(low),
                grad_input_ssm.astype(low),
                grad_query.astype(low),
                shared,
                grad_step.astype(low),
            ],
            1,
        )
    )
    mix_paired, mlp_sum_pack, out_sum_pack = lax.optimization_barrier(
        (mix_paired, mlp_sum_pack, out_sum_pack)
    )
    mix_sum_pack = reduce_far(mix_paired)
    mlp_sums = take(mlp_sum_pack, (unit_count,) * 3)
    attention_sum, mamba_out_sum = take(out_sum_pack, (query_width, scan_width))
    gate_ssm_sum, input_ssm_sum, query_sum, shared_sum, step_sum = take(
        mix_sum_pack,
        (scan_width, scan_width, query_width, shared_width // tensor_size, scan_heads),
    )
    shared_sum = shared_sum.reshape(D // count // tensor_size, shared_width)
    key_sum, value_sum, state_sum = take(
        shared_sum, (key_width, key_width, state_weight.shape[1])
    )
    mix_gain_sum = shared_sum[:, shared_width - 128]
    mlp_gain_sum = shared_sum[:, shared_width - 127]
    mix_sums = (query_sum, attention_sum, gate_ssm_sum, input_ssm_sum, step_sum, mamba_out_sum)
    shared_sums = (mix_gain_sum, mlp_gain_sum, key_sum, value_sum, state_sum)
    small_own = jnp.concatenate(
        [kernel_grad.reshape(-1), bias_grad, decay_grad, step_bias_grad, skip_grad]
    )
    small_rows = -(-small_own.shape[0] // 1024) * 8
    small_own = jnp.pad(small_own, (0, small_rows * 128 - small_own.shape[0]))
    small_every = gather_dp(small_own.reshape(small_rows, 128))
    small_sum = jnp.sum(small_every.reshape(count, small_rows, 128), 0)
    small_tensor = lax.all_gather(small_sum, "tensor", axis=0, tiled=True)
    small_tensor = small_tensor.reshape(tensor_size, -1)
    local_width = kernel_grad.shape[1]
    taps = small_tensor[:, : KCONV * local_width].reshape(tensor_size, KCONV, local_width)
    bias_start = KCONV * local_width
    biases = small_tensor[:, bias_start : bias_start + local_width]
    small_sums = [
        jnp.concatenate(
            [
                taps[:, :, :scan_width].transpose(1, 0, 2).reshape(KCONV, full_width),
                jnp.sum(taps[:, :, scan_width:], 0),
            ],
            1,
        ),
        jnp.concatenate([biases[:, :scan_width].reshape(-1), jnp.sum(biases[:, scan_width:], 0)]),
    ]
    start = bias_start + local_width
    for _ in range(3):
        small_sums.append(small_tensor[:, start : start + scan_heads].reshape(-1))
        start += scan_heads
    return (
        output,
        grad_inputs,
        shared_sums[0],
        mix_sums[0],
        shared_sums[2],
        shared_sums[3],
        mix_sums[1],
        mix_sums[2],
        mix_sums[3],
        shared_sums[4],
        mix_sums[4],
        mix_sums[5],
        small_sums[0],
        small_sums[1],
        small_sums[2],
        small_sums[3],
        small_sums[4],
        shared_sums[1],
        mlp_sums[0],
        mlp_sums[1],
        mlp_sums[2],
    )


def solution(mesh):
    placed = (
        P(("dp", "tensor"), None),
        P(("dp", "tensor"), None),
        P("dp"),
        P("dp", "tensor"),
        P("dp", None),
        P("dp", None),
        P("dp", "tensor"),
        P("dp", "tensor"),
        P("dp", "tensor"),
        P("dp", None),
        P("dp", "tensor"),
        P("dp", "tensor"),
        P(),
        P(),
        P(),
        P(),
        P(),
        P("dp"),
        P("dp", "tensor"),
        P("dp", "tensor"),
        P("dp", "tensor"),
    )
    return jax.shard_map(
        local,
        mesh=mesh,
        in_specs=placed,
        out_specs=(
            P(("dp", "tensor"), None),
            P(("dp", "tensor"), None),
            P(("dp", "tensor")),
            P("dp", "tensor"),
            P(("dp", "tensor"), None),
            P(("dp", "tensor"), None),
            P("dp", "tensor"),
            P("dp", "tensor"),
            P("dp", "tensor"),
            P(("dp", "tensor"), None),
            P("dp", "tensor"),
            P("dp", "tensor"),
            P(),
            P(),
            P(),
            P(),
            P(),
            P(("dp", "tensor")),
            P("dp", "tensor"),
            P("dp", "tensor"),
            P("dp", "tensor"),
        ),
        check_vma=False,
    )
```
